32 devices in a mesh: seq: 16 (over z, y, x), head: 2 (over core).
Axes of the slice: x: 2, y: 2, z: 4, core: 2. Of those that a mesh axis runs over, the one named last changes fastest.
Arguments:
- tokens: bfloat16 [16384, 768], P('seq'), may hold values from -6 to 6
- mix_gain: bfloat16 [768], replicated, may hold values from 0.099609375 to 1.8984375
- mix_shift: bfloat16 [768], replicated, may hold values from -1.75 to 1.75
- query_weight: bfloat16 [768, 768], P(None, 'head'), may hold values from -0.21875 to 0.21875
- query_bias: bfloat16 [768], P('head'), may hold values from -3 to 3
- key_weight: bfloat16 [768, 768], P(None, 'head'), may hold values from -0.21875 to 0.21875
- value_weight: bfloat16 [768, 768], P(None, 'head'), may hold values from -0.21875 to 0.21875
- value_bias: bfloat16 [768], P('head'), may hold values from -3 to 3
- attn_gain: bfloat16 [768], P('head'), may hold values from 0.099609375 to 1.8984375
- attn_shift: bfloat16 [768], P('head'), may hold values from -1.75 to 1.75
- out_weight: bfloat16 [768, 768], P('head'), may hold values from -0.21875 to 0.21875
- out_bias: bfloat16 [768], replicated, may hold values from -1.75 to 1.75
- feed_gain: bfloat16 [768], P(('seq', 'head')), may hold values from 0.099609375 to 1.8984375
- feed_shift: bfloat16 [768], P(('seq', 'head')), may hold values from -1.75 to 1.75
- up_weight: bfloat16 [768, 3072], P(('seq', 'head')), may hold values from -0.21875 to 0.21875
- up_bias: bfloat16 [3072], P(('seq', 'head')), may hold values from -1.75 to 1.75
- inner_gain: bfloat16 [3072], P(('seq', 'head')), may hold values from 0.099609375 to 1.8984375
- inner_shift: bfloat16 [3072], P(('seq', 'head')), may hold values from -1.75 to 1.75
- down_weight: bfloat16 [3072, 768], P(('seq', 'head')), may hold values from -0.109375 to 0.109375
- down_bias: bfloat16 [768], P(('seq', 'head')), may hold values from -1.75 to 1.75
- cotangent: bfloat16 [16384, 768], P(('seq', 'head')), may hold values from -6 to 6
Outputs:
- output: bfloat16 [16384, 768], P(('seq', 'head'))
- tokens_grad: float32 [16384, 768], P(('seq', 'head'))
- mix_gain_grad: float32 [768], P(('seq', 'head'))
- mix_shift_grad: float32 [768], P(('seq', 'head'))
- query_weight_grad: float32 [768, 768], P('seq', 'head')
- query_bias_grad: float32 [768], P(('head', 'seq'))
- key_weight_grad: float32 [768, 768], P('seq', 'head')
- value_weight_grad: float32 [768, 768], P('seq', 'head')
- value_bias_grad: float32 [768], P(('head', 'seq'))
- attn_gain_grad: float32 [768], P(('head', 'seq'))
- attn_shift_grad: float32 [768], P(('head', 'seq'))
- out_weight_grad: float32 [768, 768], P('head', 'seq')
- out_bias_grad: float32 [768], P(('seq', 'head'))
- feed_gain_grad: float32 [768], P(('seq', 'head'))
- feed_shift_grad: float32 [768], P(('seq', 'head'))
- up_weight_grad: float32 [768, 3072], P(('seq', 'head'))
- up_bias_grad: float32 [3072], P(('seq', 'head'))
- inner_gain_grad: float32 [3072], P(('seq', 'head'))
- inner_shift_grad: float32 [3072], P(('seq', 'head'))
- down_weight_grad: float32 [3072, 768], P(('seq', 'head'))
- down_bias_grad: float32 [768], P(('seq', 'head'))
The draws below stay inside these ranges and needn't reach their ends.
All inputs are finite; a program needn't handle non-finite values.
Results may differ from the reference program's by a relative error of at most 0.017.
Values may be sent and summed in bfloat16 or wider, within the bound.
No kernel may reach another device: no remote copies, remote signals or barrier semaphores. Data moves between devices by JAX's collectives and lax.ppermute only.
A program may use at most 384 MiB of HBM per device.

```python
import jax
import jax.numpy as jnp
from jax import lax

D = 768
HEADS = 12
HEAD_DIM = 64
FF = 3072
W0 = 2048
SEQ_LEN = 16384


def level_of(rng, extent, cuts, smallest, top_value):
    loudness = 1.0
    for dim, shards_of in cuts:
        steps = jax.random.uniform(jax.random.fold_in(jax.random.fold_in(rng, 6), dim), (shards_of,), jnp.float32, smallest / len(cuts), top_value / len(cuts))
        loudness = loudness * jnp.repeat(jnp.exp(steps), extent[dim] // shards_of).reshape((-1,) + (1,) * (len(extent) - 1 - dim))
    return loudness


def centred(key, extent, width, bound, cuts=(), dtype=jnp.bfloat16):
    loudness = level_of(key, extent, cuts, -0.22, 0.18) if cuts else 1.0
    values = jax.random.normal(key, extent, jnp.float32) * width * loudness
    return jnp.minimum(jnp.maximum(values, -bound), bound).astype(dtype)


def setup_inputs(seed: int = 0) -> dict:
    key_list = jax.random.split(jax.random.key(seed), 22)
    tokens = centred(key_list[0], (SEQ_LEN, D), 1.0, 6.0, ((0, 16),))
    mix_gain = jnp.clip(1.0 + 0.18 * jax.random.normal(key_list[1], (D,), jnp.float32), 0.099609375, 1.8984375).astype(jnp.bfloat16)
    mix_shift = centred(key_list[2], (D,), 0.3, 1.75)
    query_weight = centred(key_list[3], (D, D), D ** -0.5, 0.21875, ((1, 2),))
    query_bias = centred(key_list[4], (D,), 0.5, 3.0, ((0, 2),))
    key_weight = centred(key_list[5], (D, D), D ** -0.5, 0.21875, ((1, 2),))
    value_weight = centred(key_list[6], (D, D), D ** -0.5, 0.21875, ((1, 2),))
    value_bias = centred(key_list[7], (D,), 0.5, 3.0, ((0, 2),))
    attn_gain = jnp.clip(1.0 + 0.18 * jax.random.normal(key_list[8], (D,), jnp.float32), 0.099609375, 1.8984375).astype(jnp.bfloat16)
    attn_shift = centred(key_list[9], (D,), 0.3, 1.75, ((0, 2),))
    out_weight = centred(key_list[10], (D, D), D ** -0.5, 0.21875, ((0, 2),))
    out_bias = centred(key_list[11], (D,), 0.3, 1.75)
    feed_gain = jnp.clip(1.0 + 0.18 * jax.random.normal(key_list[12], (D,), jnp.float32), 0.099609375, 1.8984375).astype(jnp.bfloat16)
    feed_shift = centred(key_list[13], (D,), 0.3, 1.75, ((0, 32),))
    up_weight = centred(key_list[14], (D, FF), D ** -0.5, 0.21875, ((0, 32),))
    up_bias = centred(key_list[15], (FF,), 0.3, 1.75, ((0, 32),))
    inner_gain = jnp.clip(1.0 + 0.18 * jax.random.normal(key_list[16], (FF,), jnp.float32), 0.099609375, 1.8984375).astype(jnp.bfloat16)
    inner_shift = centred(key_list[17], (FF,), 0.3, 1.75, ((0, 32),))
    down_weight = centred(key_list[18], (FF, D), FF ** -0.5, 0.109375, ((0, 32),))
    down_bias = centred(key_list[19], (D,), 0.3, 1.75, ((0, 32),))
    cotangent = centred(key_list[20], (SEQ_LEN, D), 1.0, 6.0, ((0, 32),))
    return {"tokens": tokens, "mix_gain": mix_gain, "mix_shift": mix_shift, "query_weight": query_weight, "query_bias": query_bias, "key_weight": key_weight, "value_weight": value_weight, "value_bias": value_bias, "attn_gain": attn_gain, "attn_shift": attn_shift, "out_weight": out_weight, "out_bias": out_bias, "feed_gain": feed_gain, "feed_shift": feed_shift, "up_weight": up_weight, "up_bias": up_bias, "inner_gain": inner_gain, "inner_shift": inner_shift, "down_weight": down_weight, "down_bias": down_bias, "cotangent": cotangent}


@jax.custom_vjp
def low(v):
    return lax.optimization_barrier(v.astype(jnp.bfloat16)).astype(jnp.float32)

@jax.custom_vjp
def low_back(v):
    return v

def low_keep(v):
    return (low(v), None)

def low_pass(kept, grad):
    return (grad,)

def back_keep(v):
    return (v, None)

def back_low(kept, grad):
    return (low(grad),)
low.defvjp(low_keep, low_pass)
low_back.defvjp(back_keep, back_low)
dilation_rates = (1, 2, 4, 6, 12)
norm_eps = 1e-05
neg_big = -1e+30

def matmul(left_side, right_side):
    return jnp.dot(left_side, right_side, precision=lax.Precision.HIGHEST)

def layer_norm(values, gain, shift):
    center = lax.optimization_barrier(jnp.mean(values, axis=-1, keepdims=True))
    centered = values - center
    spread = lax.optimization_barrier(jnp.mean(centered * centered, axis=-1, keepdims=True))
    return centered * lax.rsqrt(spread + norm_eps) * gain + shift

def segment_attention(block):
    query_block, key_block, value_block = block
    count_rows = query_block.shape[0]
    scores = low_back(matmul(query_block, key_block.T) * HEAD_DIM ** (-0.5))
    causal = jnp.arange(count_rows)[:, None] >= jnp.arange(count_rows)[None, :]
    masked = jnp.where(causal, scores, neg_big)
    row_lse = jax.nn.logsumexp(masked, axis=1)
    weights_low = low(jnp.where(causal, jnp.exp(masked - row_lse[:, None]), 0.0))
    return (low_back(matmul(weights_low, value_block)), row_lse)

def dilated_head(query_head, key_head, value_head, head_idx, length):
    out_list = []
    lse_list = []
    for level_idx in range(len(dilation_rates)):
        stride = dilation_rates[level_idx]
        window_len = min(W0 * 2 ** level_idx, length)
        segments = length // window_len
        offset = head_idx % stride

        def select(source):
            return source.reshape(segments, window_len, source.shape[-1])[:, offset::stride]
        result, row_lse = lax.map(jax.checkpoint(segment_attention), (select(query_head), select(key_head), select(value_head)))
        full_out = jnp.zeros((segments, window_len, query_head.shape[-1]), jnp.float32).at[:, offset::stride].set(result)
        full_lse = jnp.full((segments, window_len), neg_big, jnp.float32).at[:, offset::stride].set(row_lse)
        out_list.append(full_out.reshape(length, query_head.shape[-1]))
        lse_list.append(full_lse.reshape(length))
    lse_stack = jnp.stack(lse_list)
    lse_total = jax.nn.logsumexp(lse_stack, axis=0)
    weights_all = jnp.exp(lse_stack - lse_total[None])
    return lax.optimization_barrier(jnp.sum(weights_all[:, :, None] * jnp.stack(out_list), axis=0))

def forward(tokens, mix_gain, mix_shift, query_weight, query_bias, key_weight, value_weight, value_bias, attn_gain, attn_shift, out_weight, out_bias, feed_gain, feed_shift, up_weight, up_bias, inner_gain, inner_shift, down_weight, down_bias):
    length = tokens.shape[0]
    normed = low(layer_norm(tokens, mix_gain, mix_shift))
    queries = low(low_back(matmul(normed, query_weight) + query_bias))
    keys_all = low(low_back(matmul(normed, key_weight)))
    values_all = low(low_back(matmul(normed, value_weight) + value_bias))
    head_outs = []
    for head_idx in range(HEADS):
        columns = slice(head_idx * HEAD_DIM, (head_idx + 1) * HEAD_DIM)
        head_outs.append(dilated_head(queries[:, columns], keys_all[:, columns], values_all[:, columns], head_idx, length))
    mixed = low(layer_norm(jnp.concatenate(head_outs, axis=1), attn_gain, attn_shift))
    branch = low_back(matmul(mixed, out_weight) + out_bias)
    hidden = tokens + branch
    feed_in = low(layer_norm(hidden, feed_gain, feed_shift))
    before = low_back(matmul(feed_in, up_weight) + up_bias)
    inner = low(layer_norm(jax.nn.gelu(before, approximate=False), inner_gain, inner_shift))
    return hidden + matmul(inner, down_weight) + down_bias

def reference(tokens, mix_gain, mix_shift, query_weight, query_bias, key_weight, value_weight, value_bias, attn_gain, attn_shift, out_weight, out_bias, feed_gain, feed_shift, up_weight, up_bias, inner_gain, inner_shift, down_weight, down_bias, cotangent):
    params = tuple((member.astype(jnp.float32) for member in (tokens, mix_gain, mix_shift, query_weight, query_bias, key_weight, value_weight, value_bias, attn_gain, attn_shift, out_weight, out_bias, feed_gain, feed_shift, up_weight, up_bias, inner_gain, inner_shift, down_weight, down_bias)))
    result, pullback = jax.vjp(forward, *params)
    gradients = pullback(cotangent.astype(jnp.float32))
    return (result.astype(jnp.bfloat16), gradients[0], gradients[1], gradients[2], gradients[3], gradients[4], gradients[5], gradients[6], gradients[7], gradients[8], gradients[9], gradients[10], gradients[11], gradients[12], gradients[13], gradients[14], gradients[15], gradients[16], gradients[17], gradients[18], gradients[19])
```

```python
import functools

import jax
import jax.numpy as jnp
from jax import lax
from jax.experimental import pallas as pl
from jax.experimental.pallas import tpu as pltpu
from jax.sharding import PartitionSpec as P

HEAD_DIM = 64
W0 = 2048
RATES = (1, 2, 4, 6, 12)
EPS = 1e-05
NEG = -1e30
CHUNK = 256
BF = jnp.bfloat16
F32 = jnp.float32
VMEM_LIMIT = 56 * 2**20
LSE_ROW = 33
HALF = HEAD_DIM
BOTH = ("seq", "head")


def layer_norm(values, gain, shift):
    center = jnp.mean(values, axis=-1, keepdims=True)
    centered = values - center
    spread = jnp.mean(centered * centered, axis=-1, keepdims=True)
    return centered * lax.rsqrt(spread + EPS) * gain + shift


def gelu_norm(before, gain, shift):
    return layer_norm(jax.nn.gelu(before, approximate=False), gain, shift)


def dot_rows(left_side, right_side):
    return lax.dot_general(
        left_side, right_side, (((0,), (0,)), ((), ())), preferred_element_type=F32
    )


def dot_cols(left_side, right_side):
    return lax.dot_general(
        left_side, right_side, (((1,), (1,)), ((), ())), preferred_element_type=F32
    )


def mm(left_side, right_side):
    return jnp.dot(left_side, right_side, preferred_element_type=F32)


class Space:
    def __init__(self, stride, levels, window):
        self.stride = stride
        self.levels = levels
        self.factor = stride if stride == 2 else stride // 2
        self.base = window if stride == 2 else window // 2
        span = CHUNK if self.factor == 2 else 128 * self.factor
        self.chunks = []
        start, rows = 0, 0
        while start < self.base:
            size = min(span, self.base - start)
            real = -(-size // self.factor)
            self.chunks.append((start, size, rows, min(128, -(-real // 16) * 16)))
            rows += 128
            start += size
        self.queries = rows
        self.keys = rows - 128 + self.chunks[-1][3]


class Plan:
    def __init__(self, tok_rows, seq_count):
        self.window = 2 * tok_rows
        windows = seq_count // 2
        self.spans = [min(2**k, windows) for k in range(len(RATES))]
        self.fold = self.spans[3] == self.spans[4]
        self.seq_count = seq_count
        top = windows.bit_length() - 1
        lists = {2: [1], 4: [2], 6: [2, 3]}
        if not self.fold:
            lists[12] = [3, 4]
        lists = {s: [b for b in bs if b <= top] for s, bs in lists.items()}
        self.spaces = [Space(s, bs, self.window) for s, bs in lists.items() if bs]
        self.levels = sorted({b for s in self.spaces for b in s.levels})
        self.packet = {}
        for level in self.levels:
            parts, at = [], 0
            for space in self.spaces:
                if level in space.levels:
                    parts.append((space.stride, at))
                    at += space.keys
            self.packet[level] = (dict(parts), at)

    def space(self, stride):
        return [s for s in self.spaces if s.stride == stride][0]

    def masks(self, level):
        found = [0]
        for bit in reversed(range(level - 1)):
            found = found + [m | (1 << bit) for m in found]
        return found


def first_of(plan, stride, window_index, heads):
    if stride == 2:
        return heads % 2
    if stride == 4:
        return heads % 4
    span = plan.spans[RATES.index(stride)]
    into = (window_index % span) * plan.window
    return jnp.mod(heads - into, stride)


def flags_at(plan, window_index, heads, place):
    code = jnp.zeros(place.shape, jnp.int32)
    for bit, stride in enumerate((2, 4, 6, 12)):
        first = first_of(plan, stride, window_index, heads)[:, None]
        code = code + jnp.where(jnp.mod(place - first, stride) == 0, 1 << bit, 0)
    return code


def weight_log(code_here, code_there, plan, stride):
    both = code_here & code_there
    f4, f6, f12 = [jnp.where((both & b) > 0, 1.0, 0.0) for b in (2, 4, 8)]
    if stride == 1:
        total = 1.0 + jnp.where((both & 1) > 0, 1.0, 0.0) + f4 + f6 + f12
    elif stride == 2:
        total = 1.0 + f4 + f6 + f12
    elif stride == 4:
        total = 1.0 + f12
    elif stride == 6 and plan.fold:
        total = 1.0 + f12
    else:
        total = jnp.ones_like(f12)
    return jnp.log(total)


def places(plan, stride, count, window_index, heads):
    steps = jnp.arange(count, dtype=jnp.int32)[None, :]
    if stride == 1:
        return jnp.broadcast_to(steps, (heads.shape[0], count))
    return first_of(plan, stride, window_index, heads)[:, None] + stride * steps


def extra_keys(plan, stride, count, window_index, heads, on):
    place = places(plan, stride, count, window_index, heads)
    code = flags_at(plan, window_index, heads, place)[:, :, None]
    bad = ((place >= plan.window) | jnp.logical_not(on))[:, :, None]
    lane = lax.broadcasted_iota(jnp.int32, (1, 1, 2 * HALF), 2) - HALF
    hot = (lane >= 0) & (lane < 32) & ((lane & 15) == code)
    hot = hot | ((lane == 32) & bad) | ((lane >= LSE_ROW) & (lane < LSE_ROW + 3))
    return jnp.where(hot, 1.0, 0.0).astype(BF)


def extra_queries(plan, stride, count, window_index, heads):
    place = places(plan, stride, count, window_index, heads)
    code = flags_at(plan, window_index, heads, place)[:, None, :]
    row = lax.broadcasted_iota(jnp.int32, (1, HALF, 1), 1)
    value = weight_log(code, row & 15, plan, stride)
    high = lax.reduce_precision(value, 8, 7)
    out = jnp.where(row < 16, high, jnp.where(row < 32, value - high, 0.0))
    return jnp.where(row == 32, NEG, out).astype(BF)


def hot_rows(count, size, factor, first):
    row = lax.broadcasted_iota(jnp.int32, (count, size), 0)
    col = lax.broadcasted_iota(jnp.int32, (count, size), 1)
    return jnp.where(col == factor * row + first, 1.0, 0.0).astype(BF)


def hot_cols(size, count, factor, first):
    row = lax.broadcasted_iota(jnp.int32, (size, count), 0)
    col = lax.broadcasted_iota(jnp.int32, (size, count), 1)
    return jnp.where(row == factor * col + first, 1.0, 0.0).astype(BF)


def lanes_down(space, first, array):
    parts = []
    hot = {}
    for start, size, at, real in space.chunks:
        if size not in hot:
            hot[size] = hot_cols(size, 128, space.factor, first)
        parts.append(mm(array[:, start : start + size], hot[size]))
    return jnp.concatenate(parts, axis=1)


def lanes_up(space, first, array):
    parts = []
    hot = {}
    for start, size, at, real in space.chunks:
        if size not in hot:
            hot[size] = hot_rows(128, size, space.factor, first)
        parts.append(mm(array[:, at : at + 128], hot[size]))
    return jnp.concatenate(parts, axis=1)


def rows_down(space, first, array):
    parts = []
    for start, size, at, real in space.chunks:
        hot = hot_rows(real, size, space.factor, first)
        parts.append(mm(hot, array[start : start + size]))
    return jnp.concatenate(parts, axis=0)


def rows_up(space, first, array):
    parts = []
    for start, size, at, real in space.chunks:
        hot = hot_cols(size, real, space.factor, first)
        parts.append(mm(hot, array[at : at + real]))
    return jnp.concatenate(parts, axis=0)


def split_two(values):
    high = values.astype(BF)
    return high, (values - high.astype(F32)).astype(BF)


def thirds(values):
    high = values.astype(BF).astype(F32)
    rest = values - high
    middle = rest.astype(BF).astype(F32)
    return high, middle, rest - middle


def stat_rows(values, rows):
    high, middle, low = thirds(values)
    row = lax.broadcasted_iota(jnp.int32, (rows, values.shape[1]), 0)
    out = jnp.where(row == 0, high, jnp.where(row == 1, middle, jnp.where(row == 2, low, 0.0)))
    return out.astype(BF)


def stat_up(space, first, values):
    got = lanes_up(space, first, stat_rows(values, 16))
    return jnp.sum(got[0:8], axis=0, keepdims=True)


def stat_down(space, first, values):
    got = lanes_down(space, first, stat_rows(values, 16))
    return jnp.sum(got[0:8], axis=0, keepdims=True)


def wide_up(space, first, values):
    high, low = split_two(values)
    m = values.shape[0]
    got = lanes_up(space, first, jnp.concatenate([high, low], axis=0))
    return got[:m] + got[m:]


def chosen_lanes(space, first):
    lane = lax.broadcasted_iota(jnp.int32, (1, space.base), 1)
    return lax.rem(lane - first + 2 * space.factor, space.factor) == 0


def log_add(*values):
    top = functools.reduce(jnp.maximum, values)
    return top + jnp.log(functools.reduce(jnp.add, [jnp.exp(v - top) for v in values]))


def with_extra(packet, extra):
    lane = lax.broadcasted_iota(jnp.int32, packet.shape, 1)
    return jnp.where(lane < HALF, packet, extra)


def with_ones(packet):
    lane = lax.broadcasted_iota(jnp.int32, packet.shape, 1)
    ones = jnp.where(lane < 3, 1.0, 0.0).astype(BF)
    return jnp.where(lane >= HALF, packet, ones)


def causal(scores, size):
    above = scores.shape[0] - size
    key = lax.broadcasted_iota(jnp.int32, (size, size), 0)
    query = lax.broadcasted_iota(jnp.int32, (size, size), 1)
    last = jnp.where(key <= query, scores[above:], NEG)
    return jnp.concatenate([scores[:above], last], axis=0) if above else last


def attend(keys_extra, values_turned, queries, size=0):
    scores = mm(keys_extra, queries)
    if size:
        scores = causal(scores, size)
    top = jnp.max(scores, axis=0, keepdims=True)
    weights = jnp.exp(scores - top)
    total = jnp.sum(weights, axis=0, keepdims=True)
    out = mm(values_turned, weights.astype(BF))
    return out / total, top + jnp.log(total)


def attend_back(keys_extra, values_ones, keys_turned, queries, grads, rows, size=0):
    scores = mm(keys_extra, queries)
    if size:
        scores = causal(scores, size)
    weights = jnp.exp(scores)
    steps = (weights * mm(values_ones, grads)).astype(BF)
    lane = lax.broadcasted_iota(jnp.int32, rows.shape, 1)
    zero = jnp.zeros_like(rows)
    pair = mm(steps, jnp.where(lane < HALF, rows, zero))
    pair = pair + mm(weights.astype(BF), jnp.where(lane >= HALF, rows, zero))
    return pair, mm(keys_turned, steps) * HEAD_DIM**-0.5


def first_in(facts, head, stride):
    return facts[head * 4 + (2, 4, 6, 12).index(stride)]


def project_kernel(
    plan, group, facts, tok, gain, shift, wq, bq, wkv, bkv, normed, q_out, kv_out, *packets
):
    for start in range(0, plan.window, CHUNK):
        rows = slice(start, start + CHUNK)
        values = tok[rows].astype(F32)
        center = jnp.mean(values, axis=1, keepdims=True)
        values = values - center
        spread = jnp.mean(values * values, axis=1, keepdims=True)
        low = (values * lax.rsqrt(spread + EPS) * gain[...] + shift[...]).astype(BF)
        normed[rows] = low
        pair = (mm(low, wkv[...]) + bkv[...]).astype(BF)
        turned = (dot_cols(wq[...], low) + bq[...]).astype(BF) * jnp.asarray(HEAD_DIM**-0.5, BF)
        for head in range(group):
            kv_out[head, rows] = pair[:, head * 128 : head * 128 + 128]
            q_out[head, :, rows] = turned[head * HALF : head * HALF + HALF]
    for head in range(group):
        picked = {}
        for space in plan.spaces:
            first = first_in(facts, head, space.stride)
            source = kv_out[head] if space.stride == 2 else picked[2]
            picked[space.stride] = rows_down(space, first, source).astype(BF)
        for ref, level in zip(packets, plan.levels):
            for stride, at in plan.packet[level][0].items():
                ref[head, at : at + plan.space(stride).keys] = picked[stride]


def own_kernel(plan, block, kv, extra_k, q, extra_q, out, lse):
    keys_extra = with_extra(kv[0], extra_k[0])
    values_turned = kv[0].T[HALF:]
    queries = jnp.concatenate([q[0], extra_q[0]], axis=0)
    for start in range(0, plan.window, block):
        stop = start + block
        got, stat = attend(
            keys_extra[:stop], values_turned[:, :stop], queries[:, start:stop], block
        )
        out[0, :, start:stop] = got
        lse[0, :, start:stop] = jnp.broadcast_to(stat, (8, block))


def space_sources(plan, space, refs):
    found = []
    for level in space.levels:
        at = plan.packet[level][0][space.stride]
        for ref in refs[level]:
            found.append((level, ref, at))
    return found


def space_attend(plan, space, refs, extra_k, queries, out, lse):
    packet = jnp.concatenate(
        [ref[0, at : at + space.keys] for level, ref, at in space_sources(plan, space, refs)],
        axis=0,
    )
    keys_extra = with_extra(packet, extra_k)
    values_turned = packet.T[HALF:]
    block = min(512, space.queries)
    for start in range(0, space.queries, block):
        got, stat = attend(keys_extra, values_turned, queries[:, start : start + block])
        out[:, start : start + block] = got
        lse[:, start : start + block] = jnp.broadcast_to(stat, (8, block))


def reach_flag(plan, facts, group, space):
    flags = [facts[4 * group + level - 1] for level in space.levels]
    return functools.reduce(jnp.maximum, flags)


def queries_of(plan, space, facts, head, q, extra_q, held):
    first = first_in(facts, head, space.stride)
    source = q if space.stride == 2 else held[2]
    picked = lanes_down(space, first, source).astype(BF)
    held[space.stride] = picked
    return jnp.concatenate([picked, extra_q], axis=0)


def near_kernel(plan, group, facts, q, *refs):
    space = plan.spaces[0]
    count = len(plan.masks(1))
    packets, (extra_k, extra_q, out, lse) = refs[:count], refs[count:]
    head = pl.program_id(0)
    flag = reach_flag(plan, facts, group, space)

    @pl.when(flag > 0)
    def _():
        queries = queries_of(plan, space, facts, head, q[0], extra_q[0], {})
        space_attend(plan, space, {1: packets}, extra_k[0], queries, out.at[0], lse.at[0])

    @pl.when(flag == 0)
    def _():
        out[...] = jnp.zeros_like(out)
        lse[...] = jnp.full_like(lse, NEG)


def far_kernel(plan, group, facts, q, out_own, lse_own, out_near, lse_near, *refs):
    refs = list(refs)
    packets = {}
    for level in plan.levels[1:]:
        packets[level] = [refs.pop(0) for _ in plan.masks(level)]
    spaces = plan.spaces[1:]
    extras = {s.stride: (refs.pop(0), refs.pop(0)) for s in spaces}
    combined, lse_all = refs.pop(0), refs.pop(0)
    held = {s.stride: (refs.pop(0), refs.pop(0)) for s in spaces}
    head = pl.program_id(0)
    near = plan.spaces[0]
    for space in spaces:
        out, lse = held[space.stride]
        flag = reach_flag(plan, facts, group, space)

        @pl.when(flag > 0)
        def _(space=space, out=out, lse=lse):
            extra_k, extra_q = extras[space.stride]
            picked = lanes_down(near, first_in(facts, head, 2), q[0]).astype(BF)
            queries = queries_of(plan, space, facts, head, None, extra_q[0], {2: picked})
            space_attend(plan, space, packets, extra_k[0], queries, out, lse)

        @pl.when(flag == 0)
        def _(out=out, lse=lse):
            out[...] = jnp.zeros_like(out)
            lse[...] = jnp.full_like(lse, NEG)

    firsts = {s.stride: first_in(facts, head, s.stride) for s in plan.spaces}
    stats = [lse_near[0, 0:1]]
    for space in spaces:
        first = firsts[space.stride]
        up = stat_up(space, first, held[space.stride][1][0:1])
        stats.append(jnp.where(chosen_lanes(space, first), up, NEG))
    lse_two = log_add(*stats)
    up = stat_up(near, firsts[2], lse_two)
    total = log_add(lse_own[0, 0:1], jnp.where(chosen_lanes(near, firsts[2]), up, NEG))
    lse_all[0] = jnp.broadcast_to(total, lse_all.shape[1:])
    total_two = stat_down(near, firsts[2], total)
    two = out_near[0] * jnp.exp(lse_near[0, 0:1] - total_two)
    for space in spaces:
        first = firsts[space.stride]
        out, lse = held[space.stride]
        total_here = stat_down(space, first, total_two)
        two = two + wide_up(space, first, out[...] * jnp.exp(lse[0:1] - total_here))
    combined[0] = out_own[0] * jnp.exp(lse_own[0, 0:1] - total) + wide_up(near, firsts[2], two)


def prepare_kernel(plan, group, facts, q, g, combined, lse, *refs):
    refs = list(refs)
    strides = [1] + [s.stride for s in plan.spaces]
    extras = {s: refs.pop(0) for s in strides}
    outs = {s: (refs.pop(0), refs.pop(0), refs.pop(0)) for s in strides}
    head = pl.program_id(0)
    total = -lse[0, 0:1]
    dots = -jnp.sum(g[0].astype(F32) * combined[0], axis=0, keepdims=True)
    stats = jnp.concatenate([stat_rows(total, 16), stat_rows(dots, 16)], axis=0)
    stack = jnp.concatenate([q[0], g[0], stats], axis=0)
    held = {1: stack}
    for stride in strides:
        if stride > 1:
            space = plan.space(stride)
            source = held[1] if stride == 2 else held[2]
            held[stride] = lanes_down(space, first_in(facts, head, stride), source).astype(BF)
        mine = held[stride]
        queries, grads, rows = outs[stride]
        stat = mine[2 * HALF :].astype(F32)
        extra = extras[stride][0].astype(F32)
        row = lax.broadcasted_iota(jnp.int32, extra.shape, 0)
        low = jnp.zeros_like(extra)
        for j in range(3):
            extra = jnp.where(row == LSE_ROW + j, stat[j : j + 1], extra)
            low = jnp.where(row == j, stat[16 + j : 17 + j], low)
        queries[0] = jnp.concatenate([mine[:HALF], extra.astype(BF)], axis=0)
        grads[0] = jnp.concatenate([low.astype(BF), mine[HALF : 2 * HALF]], axis=0)
        rows[0] = mine[: 2 * HALF].T


def space_back(plan, space, refs, extra_k, queries, grads, rows, out_q, out_refs):
    sources = space_sources(plan, space, refs)
    targets = space_sources(plan, space, out_refs)
    packet = jnp.concatenate([ref[0, at : at + space.keys] for level, ref, at in sources], axis=0)
    keys_extra = with_extra(packet, extra_k)
    values_ones = with_ones(packet)
    keys_turned = packet.T[:HALF]
    block = min(512, space.queries)
    pair = None
    for start in range(0, space.queries, block):
        stop = start + block
        got, turned = attend_back(
            keys_extra,
            values_ones,
            keys_turned,
            queries[:, start:stop],
            grads[:, start:stop],
            rows[start:stop],
        )
        pair = got if pair is None else pair + got
        out_q[:, start:stop] = turned
    for j, (level, ref, at) in enumerate(targets):
        ref[0, at : at + space.keys] = pair[j * space.keys : (j + 1) * space.keys].astype(BF)


def spaces_back_kernel(plan, group, spaces, levels, facts, *refs):
    refs = list(refs)
    packets = {lv: [refs.pop(0) for _ in plan.masks(lv)] for lv in levels}
    ins = {s.stride: [refs.pop(0) for _ in range(4)] for s in spaces}
    outs = {lv: [refs.pop(0) for _ in plan.masks(lv)] for lv in levels}
    out_q = {s.stride: refs.pop(0) for s in spaces}
    for space in spaces:
        flag = reach_flag(plan, facts, group, space)

        @pl.when(flag > 0)
        def _(space=space):
            extra_k, queries, grads, rows = [r[0] for r in ins[space.stride]]
            space_back(
                plan,
                space,
                packets,
                extra_k,
                queries,
                grads,
                rows,
                out_q[space.stride].at[0],
                outs,
            )

        @pl.when(flag == 0)
        def _(space=space):
            out_q[space.stride][...] = jnp.zeros_like(out_q[space.stride])
            for level, ref, at in space_sources(plan, space, outs):
                ref[0, at : at + space.keys] = jnp.zeros((space.keys, 128), BF)


def own_back_kernel(plan, block, kv, extra_k, queries, grads, rows, pair, out_q):
    keys_extra = with_extra(kv[0], extra_k[0])
    values_ones = with_ones(kv[0])
    keys_turned = kv[0].T[:HALF]
    for start in reversed(range(0, plan.window, block)):
        stop = start + block
        got, turned = attend_back(
            keys_extra[:stop],
            values_ones[:stop],
            keys_turned[:, :stop],
            queries[0, :, start:stop],
            grads[0, :, start:stop],
            rows[0, start:stop],
            block,
        )
        if stop == plan.window:
            pair[0] = got
        else:
            pair[0, :stop] += got
        out_q[0, :, start:stop] = turned


def gather_kernel(plan, group, facts, pair, own_q, *refs):
    refs = list(refs)
    queries = {s.stride: refs.pop(0) for s in plan.spaces}
    returns = {lv: refs.pop(0) for lv in plan.levels}
    out_pair, out_q = refs
    head = pl.program_id(0)
    near = plan.spaces[0]
    rows_two = jnp.zeros((near.keys, 128), F32)
    lanes_two = queries[2][0]
    for space in plan.spaces:
        first = first_in(facts, head, space.stride)
        total = None
        for level in space.levels:
            at = plan.packet[level][0][space.stride]
            got = returns[level][0, at : at + space.keys]
            if space.stride == 2:
                rows_two = rows_two + got.astype(F32)
            else:
                rows_two = rows_two + rows_up(space, first, got)
        if space.stride != 2:
            lanes_two = lanes_two + wide_up(space, first, queries[space.stride][0])
    first = first_in(facts, head, 2)
    high, low = split_two(rows_two)
    got = rows_up(near, first, jnp.concatenate([high, low], axis=1))
    out_pair[...] = (pair[0] + got[:, :128] + got[:, 128:]).astype(BF)
    out_q[0] = (own_q[0] + wide_up(near, first, lanes_two)).astype(BF)


def per_head(rows, cols):
    return pl.BlockSpec((1, rows, cols), lambda h: (h, 0, 0))


def head_call(kernel, group, facts, ins, outs, scratch=(), cost=0, specs=None):
    in_specs = [per_head(*a.shape[1:]) for a in ins]
    out_specs = [per_head(r, c) for r, c, d in outs]
    shapes = [jax.ShapeDtypeStruct((group, r, c), d) for r, c, d in outs]
    for j, (spec, shape) in (specs or {}).items():
        out_specs[j], shapes[j] = spec, shape
    moved = sum(a.size * a.dtype.itemsize for a in ins)
    front = [] if facts is None else [facts]
    return pl.pallas_call(
        kernel,
        grid=(group,),
        in_specs=[pl.BlockSpec(memory_space=pltpu.SMEM)] * len(front) + in_specs,
        out_specs=out_specs,
        out_shape=shapes,
        scratch_shapes=list(scratch),
        compiler_params=pltpu.CompilerParams(vmem_limit_bytes=VMEM_LIMIT),
        cost_estimate=pl.CostEstimate(flops=cost, bytes_accessed=moved, transcendentals=0),
    )(*front, *ins)


def swap(array, axis, bit, only=lambda i: True):
    count = lax.axis_size(axis)
    return lax.ppermute(array, axis, [(i, i ^ bit) for i in range(count) if only(i)])


def level_send(plan, level, packet):
    step = 1 << level
    pairs = [(i, i + step) for i in range(plan.seq_count) if not i & step]
    found = [lax.ppermute(packet, "seq", pairs)]
    for bit in reversed(range(level - 1)):
        found = found + [swap(f, "seq", 2 << bit, lambda i: i & step) for f in found]
    return found


def level_return(plan, level, grads):
    step = 1 << level
    for bit in range(level - 1):
        half = len(grads) // 2
        got = [swap(g, "seq", 2 << bit, lambda i: i & step) for g in grads[half:]]
        grads = [(a.astype(F32) + b.astype(F32)).astype(BF) for a, b in zip(grads[:half], got)]
    pairs = [(i + step, i) for i in range(plan.seq_count) if not i & step]
    return lax.ppermute(grads[0], "seq", pairs)


def in_order(bit, mine, other, axis):
    zero = bit == 0
    first = jnp.where(zero, mine, other)
    second = jnp.where(zero, other, mine)
    return jnp.concatenate([first, second], axis=axis)


def pick_half(array, index, axis):
    half = array.shape[axis] // 2
    return lax.dynamic_slice_in_dim(array, index * half, half, axis)


def per_device(
    tokens,
    mix_gain,
    mix_shift,
    query_weight,
    query_bias,
    key_weight,
    value_weight,
    value_bias,
    attn_gain,
    attn_shift,
    out_weight,
    out_bias,
    feed_gain,
    feed_shift,
    up_weight,
    up_bias,
    inner_gain,
    inner_shift,
    down_weight,
    down_bias,
    cotangent,
):
    tok_rows, width = tokens.shape
    seq_count = lax.axis_size("seq")
    devices = seq_count * lax.axis_size("head")
    plan = Plan(tok_rows, seq_count)
    seq_index = lax.axis_index("seq")
    core = lax.axis_index("head")
    cross = seq_index % 2
    window_index = seq_index // 2
    heads_here = query_weight.shape[1] // HEAD_DIM
    group = heads_here // 2
    cols = group * HEAD_DIM
    half_rows = tok_rows // 2
    heads = core * heads_here + cross * group + jnp.arange(group, dtype=jnp.int32)
    ff = up_weight.shape[1]

    up_rows = up_weight.shape[0]
    fold = ff // width
    down_rows = down_weight.shape[0]
    small = jnp.concatenate([up_bias, inner_gain, inner_shift, feed_gain, feed_shift, down_bias])
    small_at = [down_rows, down_rows, down_rows, up_rows, up_rows, up_rows]
    pad = -small.shape[0] % width
    small_rows = jnp.pad(small, (0, pad)).reshape(-1, width)
    up_packed = jnp.concatenate(
        [up_weight[:, j * width : (j + 1) * width] for j in range(fold)], axis=0
    )
    packed = jnp.concatenate([up_packed, down_weight, small_rows], axis=0)
    packed = jnp.pad(packed, ((0, -packed.shape[0] % 16), (0, 0)))
    gathered = lax.all_gather(packed, BOTH, axis=0, tiled=False)

    got = swap(pick_half(tokens, core, 0), "seq", 1)
    other = swap(got, "head", 1)
    partner = in_order(core, got, other, 0)
    window_tokens = in_order(cross, tokens, partner, 0)
    out_extra = jnp.concatenate([attn_gain, attn_shift]).reshape(1, width)
    out_packed = jnp.concatenate([out_weight, jnp.pad(out_extra, ((0, 15), (0, 0)))], axis=0)
    out_other = swap(out_packed, "head", 1)
    out_full = in_order(core, out_packed[: width // 2], out_other[: width // 2], 0)
    gain_mine, gain_other = out_packed[width // 2], out_other[width // 2]
    attn_gain_full = in_order(core, gain_mine[: width // 2], gain_other[: width // 2], 0)
    attn_shift_full = in_order(core, gain_mine[width // 2 :], gain_other[width // 2 :], 0)

    firsts = [first_of(plan, s, window_index, heads) for s in (2, 4, 6, 12)]
    firsts = [firsts[0]] + [jnp.mod(f - firsts[0], s) // 2 for f, s in zip(firsts[1:], (4, 6, 12))]
    flags = jnp.stack([(window_index >> b) & 1 for b in range(4)])
    facts = jnp.concatenate([jnp.stack(firsts, axis=1).reshape(-1), flags]).astype(jnp.int32)

    wq = pick_half(query_weight, cross, 1).T
    wk = pick_half(key_weight, cross, 1).reshape(width, group, HEAD_DIM)
    wv = pick_half(value_weight, cross, 1).reshape(width, group, HEAD_DIM)
    wkv = jnp.concatenate([wk, wv], axis=2).reshape(width, 2 * cols)
    bq = pick_half(query_bias, cross, 0).astype(F32).reshape(cols, 1)
    bv = pick_half(value_bias, cross, 0).astype(F32).reshape(group, HEAD_DIM)
    bkv = jnp.concatenate([jnp.zeros_like(bv), bv], axis=1).reshape(1, 2 * cols)
    mix_gain_wide = mix_gain.astype(F32).reshape(1, width)
    mix_shift_wide = mix_shift.astype(F32).reshape(1, width)

    whole = pl.BlockSpec(memory_space=pltpu.VMEM)
    packet_shapes = [
        jax.ShapeDtypeStruct((group, plan.packet[level][1], 128), BF) for level in plan.levels
    ]
    normed, queries_turned, pair_rows, *packets = pl.pallas_call(
        functools.partial(project_kernel, plan, group),
        in_specs=[pl.BlockSpec(memory_space=pltpu.SMEM)] + [whole] * 7,
        out_specs=[whole] * (3 + len(packet_shapes)),
        out_shape=[
            jax.ShapeDtypeStruct((plan.window, width), BF),
            jax.ShapeDtypeStruct((group, HEAD_DIM, plan.window), BF),
            jax.ShapeDtypeStruct((group, plan.window, 128), BF),
        ]
        + packet_shapes,
        compiler_params=pltpu.CompilerParams(vmem_limit_bytes=VMEM_LIMIT),
    )(facts, window_tokens, mix_gain_wide, mix_shift_wide, wq, bq, wkv, bkv)

    received = {lv: level_send(plan, lv, pk) for lv, pk in zip(plan.levels, packets)}

    on = jnp.asarray(True)
    extra_k = {1: extra_keys(plan, 1, plan.window, window_index, heads, on)}
    extra_q = {1: extra_queries(plan, 1, plan.window, window_index, heads)}
    for space in plan.spaces:
        parts = []
        for level in space.levels:
            for mask in plan.masks(level):
                source = (window_index ^ mask) ^ (1 << (level - 1))
                on = flags[level - 1] == 1
                parts.append(extra_keys(plan, space.stride, space.keys, source, heads, on))
        extra_k[space.stride] = jnp.concatenate(parts, axis=1)
        extra_q[space.stride] = extra_queries(
            plan, space.stride, space.queries, window_index, heads
        )

    window = plan.window
    near, far = plan.spaces[0], plan.spaces[1:]
    block = 512
    out_own, lse_own = head_call(
        functools.partial(own_kernel, plan, block),
        group,
        None,
        [pair_rows, extra_k[1], queries_turned, extra_q[1]],
        [(HEAD_DIM, window, F32), (8, window, F32)],
        cost=4 * group * window * window * 128,
    )
    out_near, lse_near = head_call(
        functools.partial(near_kernel, plan, group),
        group,
        facts,
        [queries_turned, *received[1], extra_k[2], extra_q[2]],
        [(HEAD_DIM, near.queries, F32), (8, near.queries, F32)],
        cost=2 * group * window * window * 128,
    )
    far_packets = [r for lv in plan.levels[1:] for r in received[lv]]
    far_extras = [e for s in far for e in (extra_k[s.stride], extra_q[s.stride])]
    scratch = []
    for s in far:
        scratch += [pltpu.VMEM((HEAD_DIM, s.queries), F32), pltpu.VMEM((8, s.queries), F32)]
    combined, lse_all = head_call(
        functools.partial(far_kernel, plan, group),
        group,
        facts,
        [queries_turned, out_own, lse_own, out_near, lse_near, *far_packets, *far_extras],
        [(HEAD_DIM, window, F32), (8, window, F32)],
        scratch,
        cost=2 * group * window * window * 128,
    )

    mixed_low = combined.reshape(cols, window).astype(BF)
    got = swap(pick_half(mixed_low, 1 - cross, 1), "seq", 1)
    joined = in_order(cross, pick_half(mixed_low, cross, 1), got, 0)
    got = swap(pick_half(joined, 1 - core, 1), "head", 1)
    joined = in_order(core, pick_half(joined, core, 1), got, 0)

    mixed_wide = joined.astype(F32).T
    attn_gain_wide = attn_gain_full.astype(F32)
    normal_wide, attn_pull = jax.vjp(
        layer_norm, mixed_wide, attn_gain_wide, attn_shift_full.astype(F32)
    )
    mixed = normal_wide.astype(BF)
    tokens_half = pick_half(tokens, core, 0).astype(F32)
    hidden = tokens_half + mm(mixed, out_full) + out_bias.astype(F32)

    up_full = jnp.concatenate(
        [
            gathered[:, j * up_rows : (j + 1) * up_rows].reshape(width, width)
            for j in range(fold)
        ],
        axis=1,
    )
    down_at = fold * up_rows
    down_full = gathered[:, down_at : down_at + down_rows].reshape(ff, width)
    small_full = gathered[:, down_at + down_rows : down_at + down_rows + small_rows.shape[0]]
    small_full = small_full.reshape(devices, -1).astype(F32)
    pieces, at = [], 0
    for size in small_at:
        pieces.append(small_full[:, at : at + size].reshape(-1))
        at += size
    up_bias_w, inner_gain_w, inner_shift_w, feed_gain_w, feed_shift_w, down_bias_w = pieces

    feed_wide, feed_pull = jax.vjp(layer_norm, hidden, feed_gain_w, feed_shift_w)
    feed_in = feed_wide.astype(BF)
    before = mm(feed_in, up_full) + up_bias_w
    inner_wide, inner_pull = jax.vjp(gelu_norm, before, inner_gain_w, inner_shift_w)
    inner = inner_wide.astype(BF)
    output = (hidden + mm(inner, down_full) + down_bias_w).astype(BF)

    cot_wide = cotangent.astype(F32)
    down_weight_grad = dot_rows(inner, cotangent)
    down_bias_grad = jnp.sum(cot_wide, axis=0)
    inner_grad = dot_cols(cotangent, down_full)
    before_grad, inner_gain_grad, inner_shift_grad = inner_pull(inner_grad)
    before_low = before_grad.astype(BF)
    up_weight_grad = dot_rows(feed_in, before_low)
    up_bias_grad = jnp.sum(before_low.astype(F32), axis=0)
    feed_grad = dot_cols(before_low, up_full)
    hidden_norm_grad, feed_gain_grad, feed_shift_grad = feed_pull(feed_grad)
    hidden_grad = cot_wide + hidden_norm_grad
    branch_low = hidden_grad.astype(BF)
    out_bias_grad = jnp.sum(branch_low.astype(F32), axis=0)
    out_grad_turned = dot_rows(branch_low, mixed)
    mixed_grad, attn_gain_grad, attn_shift_grad = attn_pull(dot_cols(branch_low, out_full))

    out_rows = width // seq_count
    out_blocks = out_grad_turned.reshape(seq_count, 2, out_rows // 2, 2, width // 2)
    out_blocks = out_blocks.transpose(0, 3, 2, 1, 4).reshape(devices, out_rows // 2, width)
    by_device = [up_bias_grad, inner_gain_grad, inner_shift_grad, down_bias_grad]
    by_device += [feed_gain_grad, feed_shift_grad, out_bias_grad]
    by_core = [attn_gain_grad, attn_shift_grad]
    small_grads = [g.reshape(devices, -1) for g in by_device]
    small_grads += [
        g.reshape(2, seq_count, -1).transpose(1, 0, 2).reshape(devices, -1) for g in by_core
    ]
    small_sizes = [g.shape[1] for g in small_grads]
    small_grads = jnp.concatenate(small_grads, axis=1)
    small_grads = jnp.pad(small_grads, ((0, 0), (0, -small_grads.shape[1] % width)))
    small_grads = small_grads.reshape(devices, -1, width)
    up_blocks = [
        up_weight_grad[:, j * width : (j + 1) * width].reshape(devices, up_rows, width)
        for j in range(fold)
    ]
    down_blocks = down_weight_grad.reshape(devices, down_rows, width)
    stack = [b.astype(BF) for b in (*up_blocks, down_blocks, out_blocks, small_grads)]
    stack = jnp.concatenate(stack, axis=1)
    stack = jnp.pad(stack, ((0, 0), (0, -stack.shape[1] % 16), (0, 0)))
    summed = lax.psum_scatter(
        stack.reshape(-1, width), BOTH, scatter_dimension=0, tiled=True
    ).astype(F32)

    grad_turned = mixed_grad.astype(BF).T
    got = swap(pick_half(grad_turned, 1 - core, 0), "head", 1)
    joined = in_order(core, pick_half(grad_turned, core, 0), got, 1)
    got = swap(pick_half(joined, 1 - cross, 0), "seq", 1)
    joined = in_order(cross, pick_half(joined, cross, 0), got, 1)
    grads_turned = joined.reshape(group, HEAD_DIM, window)

    strides = [1] + [s.stride for s in plan.spaces]
    counts = [window] + [s.queries for s in plan.spaces]
    prepared = head_call(
        functools.partial(prepare_kernel, plan, group),
        group,
        facts,
        [queries_turned, grads_turned, combined, lse_all, *[extra_q[s] for s in strides]],
        [o for n in counts for o in ((128, n, BF), (128, n, BF), (n, 128, BF))],
    )
    prepared = {s: prepared[3 * j : 3 * j + 3] for j, s in enumerate(strides)}

    def back(spaces, levels, cost):
        ins = [r for lv in levels for r in received[lv]]
        shapes = [(r.shape[1], 128, BF) for r in ins]
        for s in spaces:
            ins += [extra_k[s.stride], *prepared[s.stride]]
        shapes += [(HEAD_DIM, s.queries, F32) for s in spaces]
        outs = head_call(
            functools.partial(spaces_back_kernel, plan, group, spaces, levels),
            group,
            facts,
            ins,
            shapes,
            cost=cost,
        )
        pairs, at = {}, 0
        for lv in levels:
            pairs[lv] = list(outs[at : at + len(received[lv])])
            at += len(received[lv])
        return pairs, list(outs[at:])

    far_pairs, far_queries = back(far, plan.levels[1:], 5 * group * window * window * 128)
    returned = {lv: level_return(plan, lv, far_pairs[lv]) for lv in plan.levels[1:]}
    near_pairs, near_queries = back([near], [1], 5 * group * window * window * 128)
    returned[1] = level_return(plan, 1, near_pairs[1])
    own_pair, own_q = head_call(
        functools.partial(own_back_kernel, plan, 256),
        group,
        None,
        [pair_rows, extra_k[1], *prepared[1]],
        [(window, 128, F32), (HEAD_DIM, window, F32)],
        cost=10 * group * window * window * 128,
    )
    pair_spec = pl.BlockSpec((window, 128), lambda h: (0, h))
    pair_shape = jax.ShapeDtypeStruct((window, group * 128), BF)
    pair_low, query_low = head_call(
        functools.partial(gather_kernel, plan, group),
        group,
        facts,
        [own_pair, own_q, *near_queries, *far_queries, *[returned[lv] for lv in plan.levels]],
        [(window, 128, BF), (HEAD_DIM, window, BF)],
        specs={0: (pair_spec, pair_shape)},
    )
    query_low = query_low.reshape(cols, window)

    part = dot_rows(query_low, wq) + dot_cols(pair_low, wkv)
    tokens_wide = window_tokens.astype(F32)
    center = jnp.mean(tokens_wide, axis=1, keepdims=True)
    centered = tokens_wide - center
    spread = jnp.mean(centered * centered, axis=1, keepdims=True)
    plain = centered * lax.rsqrt(spread + EPS)
    mix_part = jnp.concatenate([jnp.sum(part * plain, axis=0), jnp.sum(part, axis=0)])
    part_low = part.astype(BF).reshape(2, 2, half_rows, width)
    mine = lax.dynamic_index_in_dim(part_low, core, 1, keepdims=False)
    away = lax.dynamic_index_in_dim(part_low, 1 - core, 1, keepdims=False)
    got = swap(away, "head", 1)
    both = (mine.astype(F32) + got.astype(F32)).astype(BF)
    mine = lax.dynamic_index_in_dim(both, cross, 0, keepdims=False)
    away = lax.dynamic_index_in_dim(both, 1 - cross, 0, keepdims=False)
    normed_grad = mine.astype(F32) + swap(away, "seq", 1).astype(F32)
    tokens_norm_grad = jax.vjp(layer_norm, tokens_half, mix_gain.astype(F32), mix_shift.astype(F32))[
        1
    ](normed_grad)[0]
    tokens_grad = hidden_grad + tokens_norm_grad

    weight_part = jnp.concatenate(
        [dot_rows(normed, pair_low), dot_cols(normed.T, query_low)], axis=1
    ).astype(BF)
    pair_sums = jnp.sum(pair_low.astype(F32), axis=0)
    query_sums = jnp.sum(query_low.astype(F32), axis=1)
    sums = jnp.concatenate([pair_sums, query_sums, mix_part])
    sums_pad = -sums.shape[0] % 1024
    sums = jnp.pad(sums, (0, sums_pad)).reshape(-1, 128)
    block_rows = width // seq_count
    weight_part = weight_part.reshape(seq_count // 2, 2 * block_rows, 3 * cols)
    bits = (seq_count // 2).bit_length() - 1
    for bit in reversed(range(bits)):
        here = (window_index >> bit) & 1
        mine = pick_half(weight_part, here, 0)
        got = swap(pick_half(weight_part, 1 - here, 0), "seq", 2 << bit)
        weight_part = (mine.astype(F32) + got.astype(F32)).astype(BF)
        sums = sums + swap(sums, "seq", 2 << bit)
    weight_part = weight_part[0]
    got = swap(pick_half(weight_part, 1 - cross, 0), "seq", 1)
    mine = pick_half(weight_part, cross, 0)
    sums_other = swap(sums, "seq", 1)
    flat, flat_other = sums.reshape(-1), sums_other.reshape(-1)
    mix_sum = flat[3 * cols : 3 * cols + 2 * width] + flat_other[3 * cols : 3 * cols + 2 * width]
    mix_sum = mix_sum.reshape(-1, 128)
    mix_sum = (mix_sum + swap(mix_sum, "head", 1)).reshape(2, devices, -1)
    mix_sum = lax.dynamic_index_in_dim(mix_sum, seq_index * 2 + core, 1, keepdims=False)

    def parts_of(array):
        pair = array[..., : 2 * cols].reshape(array.shape[:-1] + (group, 2, HEAD_DIM))
        key, value = pair[..., 0, :], pair[..., 1, :]
        lead = array.shape[:-1] + (cols,)
        return array[..., 2 * cols : 3 * cols], key.reshape(lead), value.reshape(lead)

    weight_grads = [
        in_order(cross, a, b, 1).astype(F32) for a, b in zip(parts_of(mine), parts_of(got))
    ]
    bias_grads = [
        lax.dynamic_index_in_dim(
            in_order(cross, a, b, 0).reshape(seq_count, -1), seq_index, 0, keepdims=False
        )
        for a, b in zip(parts_of(flat[: 3 * cols]), parts_of(flat_other[: 3 * cols]))
    ]

    up_sum = jnp.concatenate(
        [summed[j * up_rows : (j + 1) * up_rows] for j in range(fold)], axis=1
    )
    at = fold * up_rows
    down_sum = summed[at : at + down_rows]
    at += down_rows
    out_sum = summed[at : at + out_rows // 2].reshape(out_rows // 2, 2, width // 2)
    out_sum = out_sum.transpose(1, 0, 2).reshape(out_rows, width // 2).T
    at += out_rows // 2
    flat_small = summed[at : at + small_grads.shape[1]].reshape(-1)
    smalls, place = [], 0
    for size in small_sizes:
        smalls.append(flat_small[place : place + size])
        place += size
    (
        up_bias_sum,
        inner_gain_sum,
        inner_shift_sum,
        down_bias_sum,
        feed_gain_sum,
        feed_shift_sum,
        out_bias_sum,
        attn_gain_sum,
        attn_shift_sum,
    ) = smalls
    return (
        output,
        tokens_grad,
        mix_sum[0],
        mix_sum[1],
        weight_grads[0],
        bias_grads[0],
        weight_grads[1],
        weight_grads[2],
        bias_grads[2],
        attn_gain_sum,
        attn_shift_sum,
        out_sum,
        out_bias_sum,
        feed_gain_sum,
        feed_shift_sum,
        up_sum,
        up_bias_sum,
        inner_gain_sum,
        inner_shift_sum,
        down_sum,
        down_bias_sum,
    )


def solution(mesh):
    return jax.shard_map(
        per_device,
        mesh=mesh,
        in_specs=(
            P("seq", None),
            P(),
            P(),
            P(None, "head"),
            P("head"),
            P(None, "head"),
            P(None, "head"),
            P("head"),
            P("head"),
            P("head"),
            P("head", None),
            P(),
            P(("seq", "head")),
            P(("seq", "head")),
            P(("seq", "head"), None),
            P(("seq", "head")),
            P(("seq", "head")),
            P(("seq", "head")),
            P(("seq", "head"), None),
            P(("seq", "head")),
            P(("seq", "head"), None),
        ),
        out_specs=(
            P(("seq", "head"), None),
            P(("seq", "head"), None),
            P(("seq", "head")),
            P(("seq", "head")),
            P("seq", "head"),
            P(("head", "seq")),
            P("seq", "head"),
            P("seq", "head"),
            P(("head", "seq")),
            P(("head", "seq")),
            P(("head", "seq")),
            P("head", "seq"),
            P(("seq", "head")),
            P(("seq", "head")),
            P(("seq", "head")),
            P(("seq", "head"), None),
            P(("seq", "head")),
            P(("seq", "head")),
            P(("seq", "head")),
            P(("seq", "head"), None),
            P(("seq", "head")),
        ),
        check_vma=False,
    )
```

```python
import functools

import jax
import jax.numpy as jnp
from jax import lax
from jax.experimental import pallas as pl
from jax.experimental.pallas import tpu as pltpu
from jax.sharding import PartitionSpec as P

HEAD_DIM = 64
W0 = 2048
RATES = (1, 2, 4, 6, 12)
EPS = 1e-05
NEG = -1e30
CHUNK = 256
BF = jnp.bfloat16
F32 = jnp.float32
VMEM_LIMIT = 56 * 2**20
LSE_ROW = 33
HALF = HEAD_DIM
BOTH = ("seq", "head")


def layer_norm(values, gain, shift):
    center = jnp.mean(values, axis=-1, keepdims=True)
    centered = values - center
    spread = jnp.mean(centered * centered, axis=-1, keepdims=True)
    return centered * lax.rsqrt(spread + EPS) * gain + shift


def dot_rows(left_side, right_side):
    return lax.dot_general(
        left_side, right_side, (((0,), (0,)), ((), ())), preferred_element_type=F32
    )


def dot_cols(left_side, right_side):
    return lax.dot_general(
        left_side, right_side, (((1,), (1,)), ((), ())), preferred_element_type=F32
    )


def mm(left_side, right_side):
    return jnp.dot(left_side, right_side, preferred_element_type=F32)


class Space:
    def __init__(self, stride, levels, window):
        self.stride = stride
        self.levels = levels
        self.factor = stride if stride == 2 else stride // 2
        self.base = window if stride == 2 else window // 2
        span = CHUNK if self.factor == 2 else 128 * self.factor
        self.chunks = []
        start, rows = 0, 0
        while start < self.base:
            size = min(span, self.base - start)
            real = -(-size // self.factor)
            self.chunks.append((start, size, rows, min(128, -(-real // 16) * 16)))
            rows += 128
            start += size
        self.queries = rows
        self.keys = rows - 128 + self.chunks[-1][3]


class Plan:
    def __init__(self, tok_rows, seq_count):
        self.window = 2 * tok_rows
        windows = seq_count // 2
        self.spans = [min(2**k, windows) for k in range(len(RATES))]
        self.fold = self.spans[3] == self.spans[4]
        self.seq_count = seq_count
        top = windows.bit_length() - 1
        lists = {2: [1], 4: [2], 6: [2, 3]}
        if not self.fold:
            lists[12] = [3, 4]
        lists = {s: [b for b in bs if b <= top] for s, bs in lists.items()}
        self.spaces = [Space(s, bs, self.window) for s, bs in lists.items() if bs]
        self.levels = sorted({b for s in self.spaces for b in s.levels})
        self.packet = {}
        for level in self.levels:
            parts, at = [], 0
            for space in self.spaces:
                if level in space.levels:
                    parts.append((space.stride, at))
                    at += space.keys
            self.packet[level] = (dict(parts), at)

    def space(self, stride):
        return [s for s in self.spaces if s.stride == stride][0]

    def masks(self, level):
        found = [0]
        for bit in reversed(range(level - 1)):
            found = found + [m | (1 << bit) for m in found]
        return found


def first_of(plan, stride, window_index, heads):
    if stride == 2:
        return heads % 2
    if stride == 4:
        return heads % 4
    span = plan.spans[RATES.index(stride)]
    into = (window_index % span) * plan.window
    return jnp.mod(heads - into, stride)


def flags_at(plan, window_index, heads, place):
    code = jnp.zeros(place.shape, jnp.int32)
    for bit, stride in enumerate((2, 4, 6, 12)):
        first = first_of(plan, stride, window_index, heads)[:, None]
        code = code + jnp.where(jnp.mod(place - first, stride) == 0, 1 << bit, 0)
    return code


def weight_log(code_here, code_there, plan, stride):
    both = code_here & code_there
    f4, f6, f12 = [jnp.where((both & b) > 0, 1.0, 0.0) for b in (2, 4, 8)]
    if stride == 1:
        total = 1.0 + jnp.where((both & 1) > 0, 1.0, 0.0) + f4 + f6 + f12
    elif stride == 2:
        total = 1.0 + f4 + f6 + f12
    elif stride == 4 and not plan.fold:
        total = 1.0 + f12
    elif stride == 6 and plan.fold:
        total = 1.0 + f12
    else:
        total = jnp.ones_like(f12)
    return jnp.log(total)


def places(plan, stride, count, window_index, heads):
    steps = jnp.arange(count, dtype=jnp.int32)[None, :]
    if stride == 1:
        return jnp.broadcast_to(steps, (heads.shape[0], count))
    return first_of(plan, stride, window_index, heads)[:, None] + stride * steps


def extra_keys(plan, stride, count, window_index, heads, on):
    place = places(plan, stride, count, window_index, heads)
    code = flags_at(plan, window_index, heads, place)[:, :, None]
    bad = ((place >= plan.window) | jnp.logical_not(on))[:, :, None]
    lane = lax.broadcasted_iota(jnp.int32, (1, 1, 2 * HALF), 2) - HALF
    hot = (lane >= 0) & (lane < 32) & ((lane & 15) == code)
    hot = hot | ((lane == 32) & bad) | ((lane >= LSE_ROW) & (lane < LSE_ROW + 3))
    return jnp.where(hot, 1.0, 0.0).astype(BF)


def extra_queries(plan, stride, count, window_index, heads):
    place = places(plan, stride, count, window_index, heads)
    code = flags_at(plan, window_index, heads, place)[:, None, :]
    row = lax.broadcasted_iota(jnp.int32, (1, HALF, 1), 1)
    value = weight_log(code, row & 15, plan, stride)
    high = lax.reduce_precision(value, 8, 7)
    out = jnp.where(row < 16, high, jnp.where(row < 32, value - high, 0.0))
    return jnp.where(row == 32, NEG, out).astype(BF)


def hot_rows(count, size, factor, first):
    row = lax.broadcasted_iota(jnp.int32, (count, size), 0)
    col = lax.broadcasted_iota(jnp.int32, (count, size), 1)
    return jnp.where(col == factor * row + first, 1.0, 0.0).astype(BF)


def hot_cols(size, count, factor, first):
    row = lax.broadcasted_iota(jnp.int32, (size, count), 0)
    col = lax.broadcasted_iota(jnp.int32, (size, count), 1)
    return jnp.where(row == factor * col + first, 1.0, 0.0).astype(BF)


def lanes_down(space, first, array):
    parts = []
    hot = {}
    for start, size, at, real in space.chunks:
        if size not in hot:
            hot[size] = hot_cols(size, 128, space.factor, first)
        parts.append(mm(array[:, start : start + size], hot[size]))
    return jnp.concatenate(parts, axis=1)


def lanes_up(space, first, array):
    parts = []
    hot = {}
    for start, size, at, real in space.chunks:
        if size not in hot:
            hot[size] = hot_rows(128, size, space.factor, first)
        parts.append(mm(array[:, at : at + 128], hot[size]))
    return jnp.concatenate(parts, axis=1)


def rows_down(space, first, array):
    parts = []
    for start, size, at, real in space.chunks:
        hot = hot_rows(real, size, space.factor, first)
        parts.append(mm(hot, array[start : start + size]))
    return jnp.concatenate(parts, axis=0)


def rows_up(space, first, array):
    parts = []
    for start, size, at, real in space.chunks:
        hot = hot_cols(size, real, space.factor, first)
        parts.append(mm(hot, array[at : at + real]))
    return jnp.concatenate(parts, axis=0)


def split_two(values):
    high = values.astype(BF)
    return high, (values - high.astype(F32)).astype(BF)


def thirds(values):
    high = values.astype(BF).astype(F32)
    rest = values - high
    middle = rest.astype(BF).astype(F32)
    return high, middle, rest - middle


def stat_rows(values, rows):
    high, middle, low = thirds(values)
    row = lax.broadcasted_iota(jnp.int32, (rows, values.shape[1]), 0)
    out = jnp.where(row == 0, high, jnp.where(row == 1, middle, jnp.where(row == 2, low, 0.0)))
    return out.astype(BF)


def stat_up(space, first, values):
    got = lanes_up(space, first, stat_rows(values, 16))
    return jnp.sum(got[0:8], axis=0, keepdims=True)


def stat_down(space, first, values):
    got = lanes_down(space, first, stat_rows(values, 16))
    return jnp.sum(got[0:8], axis=0, keepdims=True)


def wide_up(space, first, values):
    high, low = split_two(values)
    m = values.shape[0]
    got = lanes_up(space, first, jnp.concatenate([high, low], axis=0))
    return got[:m] + got[m:]


def chosen_lanes(space, first):
    lane = lax.broadcasted_iota(jnp.int32, (1, space.base), 1)
    return lax.rem(lane - first + 2 * space.factor, space.factor) == 0


def log_add(*values):
    top = functools.reduce(jnp.maximum, values)
    return top + jnp.log(functools.reduce(jnp.add, [jnp.exp(v - top) for v in values]))


def with_extra(packet, extra):
    lane = lax.broadcasted_iota(jnp.int32, packet.shape, 1)
    return jnp.where(lane < HALF, packet, extra)


def with_ones(packet):
    lane = lax.broadcasted_iota(jnp.int32, packet.shape, 1)
    ones = jnp.where(lane < 3, 1.0, 0.0).astype(BF)
    return jnp.where(lane >= HALF, packet, ones)


def causal(scores, size):
    above = scores.shape[0] - size
    key = lax.broadcasted_iota(jnp.int32, (size, size), 0)
    query = lax.broadcasted_iota(jnp.int32, (size, size), 1)
    last = jnp.where(key <= query, scores[above:], NEG)
    return jnp.concatenate([scores[:above], last], axis=0) if above else last


def attend(keys_extra, values_turned, queries, size=0):
    scores = mm(keys_extra, queries)
    if size:
        scores = causal(scores, size)
    top = jnp.max(scores, axis=0, keepdims=True)
    weights = jnp.exp(scores - top)
    total = jnp.sum(weights, axis=0, keepdims=True)
    out = mm(values_turned, weights.astype(BF))
    return out / total, top + jnp.log(total)


def attend_back(keys_extra, values_ones, keys_turned, queries, grads, rows, size=0):
    scores = mm(keys_extra, queries)
    if size:
        scores = causal(scores, size)
    weights = jnp.exp(scores)
    steps = (weights * mm(values_ones, grads)).astype(BF)
    lane = lax.broadcasted_iota(jnp.int32, rows.shape, 1)
    zero = jnp.zeros_like(rows)
    pair = mm(steps, jnp.where(lane < HALF, rows, zero))
    pair = pair + mm(weights.astype(BF), jnp.where(lane >= HALF, rows, zero))
    return pair, mm(keys_turned, steps) * HEAD_DIM**-0.5


def first_in(facts, head, stride):
    return facts[head * 4 + (2, 4, 6, 12).index(stride)]


def project_kernel(
    plan, group, facts, tok, gain, shift, wq, bq, wkv, bkv, normed, q_out, kv_out, *packets
):
    for start in range(0, plan.window, CHUNK):
        rows = slice(start, start + CHUNK)
        values = tok[rows].astype(F32)
        center = jnp.mean(values, axis=1, keepdims=True)
        values = values - center
        spread = jnp.mean(values * values, axis=1, keepdims=True)
        low = (values * lax.rsqrt(spread + EPS) * gain[...] + shift[...]).astype(BF)
        normed[rows] = low
        pair = (mm(low, wkv[...]) + bkv[...]).astype(BF)
        turned = (dot_cols(wq[...], low) + bq[...]).astype(BF) * jnp.asarray(HEAD_DIM**-0.5, BF)
        for head in range(group):
            kv_out[head, rows] = pair[:, head * 128 : head * 128 + 128]
            q_out[head, :, rows] = turned[head * HALF : head * HALF + HALF]
    for head in range(group):
        picked = {}
        for space in plan.spaces:
            first = first_in(facts, head, space.stride)
            source = kv_out[head] if space.stride == 2 else picked[2]
            picked[space.stride] = rows_down(space, first, source).astype(BF)
        for ref, level in zip(packets, plan.levels):
            for stride, at in plan.packet[level][0].items():
                ref[head, at : at + plan.space(stride).keys] = picked[stride]


def own_kernel(plan, block, kv, extra_k, q, extra_q, out, lse):
    keys_extra = with_extra(kv[0], extra_k[0])
    values_turned = kv[0].T[HALF:]
    queries = jnp.concatenate([q[0], extra_q[0]], axis=0)
    for start in range(0, plan.window, block):
        stop = start + block
        got, stat = attend(
            keys_extra[:stop], values_turned[:, :stop], queries[:, start:stop], block
        )
        out[0, :, start:stop] = got
        lse[0, :, start:stop] = jnp.broadcast_to(stat, (8, block))


def space_sources(plan, space, refs):
    found = []
    for level in space.levels:
        at = plan.packet[level][0][space.stride]
        for ref in refs[level]:
            found.append((level, ref, at))
    return found


def space_attend(plan, space, refs, extra_k, queries, out, lse):
    packet = jnp.concatenate(
        [ref[0, at : at + space.keys] for level, ref, at in space_sources(plan, space, refs)],
        axis=0,
    )
    keys_extra = with_extra(packet, extra_k)
    values_turned = packet.T[HALF:]
    block = min(512, space.queries)
    for start in range(0, space.queries, block):
        got, stat = attend(keys_extra, values_turned, queries[:, start : start + block])
        out[:, start : start + block] = got
        lse[:, start : start + block] = jnp.broadcast_to(stat, (8, block))


def reach_flag(plan, facts, group, space):
    flags = [facts[4 * group + level - 1] for level in space.levels]
    return functools.reduce(jnp.maximum, flags)


def queries_of(plan, space, facts, head, q, extra_q, held):
    first = first_in(facts, head, space.stride)
    source = q if space.stride == 2 else held[2]
    picked = lanes_down(space, first, source).astype(BF)
    held[space.stride] = picked
    return jnp.concatenate([picked, extra_q], axis=0)


def sides(facts, group):
    return facts[4 * group + 4], facts[4 * group + 5]


def swap_if(flag, first, second):
    return jnp.where(flag == 0, first, second), jnp.where(flag == 0, second, first)


def join_if(flag, mine, other, axis):
    return jnp.concatenate(swap_if(flag, mine, other), axis=axis)


def near_kernel(plan, group, facts, q, *refs):
    space = plan.spaces[0]
    count = len(plan.masks(1))
    packets, (extra_k, extra_q, out, lse) = refs[:count], refs[count:]
    head = pl.program_id(0)
    flag = reach_flag(plan, facts, group, space)

    @pl.when(flag > 0)
    def _():
        queries = queries_of(plan, space, facts, head, q[0], extra_q[0], {})
        space_attend(plan, space, {1: packets}, extra_k[0], queries, out.at[0], lse.at[0])

    @pl.when(flag == 0)
    def _():
        out[...] = jnp.zeros_like(out)
        lse[...] = jnp.full_like(lse, NEG)


def far_kernel(plan, group, facts, q, out_own, lse_own, out_near, lse_near, *refs):
    refs = list(refs)
    packets = {}
    for level in plan.levels[1:]:
        packets[level] = [refs.pop(0) for _ in plan.masks(level)]
    spaces = plan.spaces[1:]
    extras = {s.stride: (refs.pop(0), refs.pop(0)) for s in spaces}
    combined, lse_all, same, other, away = [refs.pop(0) for _ in range(5)]
    held = {s.stride: (refs.pop(0), refs.pop(0)) for s in spaces}
    head = pl.program_id(0)
    near = plan.spaces[0]
    for space in spaces:
        out, lse = held[space.stride]
        flag = reach_flag(plan, facts, group, space)

        @pl.when(flag > 0)
        def _(space=space, out=out, lse=lse):
            extra_k, extra_q = extras[space.stride]
            picked = lanes_down(near, first_in(facts, head, 2), q[0]).astype(BF)
            queries = queries_of(plan, space, facts, head, None, extra_q[0], {2: picked})
            space_attend(plan, space, packets, extra_k[0], queries, out, lse)

        @pl.when(flag == 0)
        def _(out=out, lse=lse):
            out[...] = jnp.zeros_like(out)
            lse[...] = jnp.full_like(lse, NEG)

    firsts = {s.stride: first_in(facts, head, s.stride) for s in plan.spaces}
    stats = [lse_near[0, 0:1]]
    for space in spaces:
        first = firsts[space.stride]
        up = stat_up(space, first, held[space.stride][1][0:1])
        stats.append(jnp.where(chosen_lanes(space, first), up, NEG))
    lse_two = log_add(*stats)
    up = stat_up(near, firsts[2], lse_two)
    total = log_add(lse_own[0, 0:1], jnp.where(chosen_lanes(near, firsts[2]), up, NEG))
    lse_all[0] = jnp.broadcast_to(total, lse_all.shape[1:])
    total_two = stat_down(near, firsts[2], total)
    two = out_near[0] * jnp.exp(lse_near[0, 0:1] - total_two)
    for space in spaces:
        first = firsts[space.stride]
        out, lse = held[space.stride]
        total_here = stat_down(space, first, total_two)
        two = two + wide_up(space, first, out[...] * jnp.exp(lse[0:1] - total_here))
    got = out_own[0] * jnp.exp(lse_own[0, 0:1] - total) + wide_up(near, firsts[2], two)
    combined[0] = got
    low = got.astype(BF)
    cross, core = sides(facts, group)
    half = plan.window // 2
    mine, gone = swap_if(cross, low[:, :half], low[:, half:])
    same[0], other[0] = swap_if(core, mine[:, : half // 2], mine[:, half // 2 :])
    away[0] = jnp.concatenate(swap_if(core, gone[:, : half // 2], gone[:, half // 2 :]), axis=1)


def norm_parts(values, width):
    center = jnp.sum(values, axis=1, keepdims=True) * (1.0 / width)
    centered = values - center
    spread = jnp.sum(centered * centered, axis=1, keepdims=True) * (1.0 / width)
    scale = lax.rsqrt(spread + EPS)
    return centered * scale, scale


def norm_back(grads, gain, plain, scale, width):
    up = grads * gain
    mean = jnp.sum(up, axis=1, keepdims=True) * (1.0 / width)
    cross = jnp.sum(up * plain, axis=1, keepdims=True) * (1.0 / width)
    gain_grad = jnp.sum(grads * plain, axis=0, keepdims=True)
    shift_grad = jnp.sum(grads, axis=0, keepdims=True)
    return (up - mean - plain * cross) * scale, gain_grad, shift_grad


class Shares:
    def __init__(self, devices, width, ff):
        self.devices, self.width, self.fold = devices, width, ff // width
        self.up_rows, self.down_rows = width // devices, ff // devices
        self.out_rows = 2 * width // devices
        self.up_span = -(-self.up_rows // 16) * 16
        self.down_at = 2 * self.fold * self.up_span
        self.out_at = self.down_at + 2 * self.down_rows
        self.small_at = self.out_at + self.out_rows
        self.small_size = 3 * self.down_rows + 6 * self.up_rows
        rows = self.small_at + -(-2 * self.small_size // width)
        self.rows = -(-rows // 16) * 16
        self.direct = not (self.up_rows % 8 or self.down_rows % 16 or self.out_rows % 16)

    def stack(self, up, down, out):
        half = self.width // 2
        up = up.reshape(self.fold, self.devices, self.up_rows, 2, half)
        up = jnp.pad(up, ((0, 0), (0, 0), (0, self.up_span - self.up_rows), (0, 0), (0, 0)))
        up = up.transpose(1, 0, 3, 2, 4).reshape(self.devices, -1, half)
        down = down.reshape(self.devices, self.down_rows, 2, half)
        down = down.transpose(0, 2, 1, 3).reshape(self.devices, -1, half)
        out = out.reshape(-1, self.out_rows, 2, half)
        out = out.transpose(0, 2, 1, 3).reshape(self.devices, -1, half)
        stack = jnp.concatenate([up, down, out], axis=1)
        return jnp.pad(stack, ((0, 0), (0, self.rows - stack.shape[1]), (0, 0)))

    def small(self, values):
        values = jnp.concatenate(values, axis=1)
        pad = -values.shape[1] % (self.width // 2)
        values = jnp.pad(values, ((0, 0), (0, pad)))
        return values.reshape(self.devices, -1, self.width // 2)


def feed_kernel(
    group,
    fold,
    shares,
    direct,
    facts,
    same,
    across,
    beside,
    beyond,
    tok,
    cot,
    out_w,
    up_w,
    down_w,
    narrow,
    broad,
    output,
    hidden_grad,
    gone,
    kept_away,
    kept,
    broad_g,
    narrow_g,
    *rest,
):
    *grad_refs, gelu, slope, inner_g = rest
    cross, core = sides(facts, group)
    rows, width = tok.shape
    half = width // 2

    def put_up(j, value):
        if not direct:
            grad_refs[0][j] = value.astype(BF)
            return
        stack, step, span = grad_refs[0], shares.up_rows, shares.up_span
        for device in range(shares.devices):
            piece = value[device * step : device * step + span]
            if piece.shape[0] < span:
                piece = jnp.concatenate(
                    [piece, jnp.zeros((span - piece.shape[0], width), F32)], axis=0
                )
            piece = piece.astype(BF)
            for part in range(2):
                at = pl.multiple_of((2 * j + part) * span, span)
                stack[device, pl.ds(at, span)] = piece[:, part * half : (part + 1) * half]

    def put_down(j, value):
        value = value.astype(BF)
        if not direct:
            grad_refs[1][j] = value
            return
        stack, step = grad_refs[0], shares.down_rows
        count = width // step
        for i in range(count):
            for part in range(2):
                at = shares.down_at + part * step
                stack[j * count + i, at : at + step] = value[
                    i * step : (i + 1) * step, part * half : (part + 1) * half
                ]

    def put_out(value):
        value = value.astype(BF)
        if not direct:
            grad_refs[2][...] = value
            return
        stack, step = grad_refs[0], shares.out_rows
        for device in range(shares.devices):
            i, part = device // 2, device % 2
            stack[device, shares.out_at : shares.out_at + step] = value[
                i * step : (i + 1) * step, part * half : (part + 1) * half
            ]
    cols = same.shape[0]
    ff = fold * width
    here = join_if(cross, same[...], across[:, :rows], 0)
    there = join_if(cross, beside[...], beyond[...], 0)
    combined = join_if(core, here, there, 0).T.astype(F32)
    attn_plain, attn_scale = norm_parts(combined, width)
    mixed = (attn_plain * narrow[0:1] + narrow[1:2]).astype(BF)
    hidden = tok[...].astype(F32) + mm(mixed, out_w[...]) + narrow[2:3]
    feed_plain, feed_scale = norm_parts(hidden, width)
    feed_in = (feed_plain * narrow[3:4] + narrow[4:5]).astype(BF)

    def forward(j, total):
        before = mm(feed_in, up_w[j]) + broad[0, j]
        phi = 0.5 + 0.5 * lax.erf(before * 0.5**0.5)
        value = before * phi
        gelu[j] = value
        slope[j] = phi + before * jnp.exp(before * before * -0.5) * (2.0 * jnp.pi) ** -0.5
        return total + jnp.sum(value, axis=1, keepdims=True)

    zero = jnp.zeros((rows, 1), F32)
    center = lax.fori_loop(0, fold, forward, zero) * (1.0 / ff)

    def squares(j, total):
        value = gelu[j] - center
        return total + jnp.sum(value * value, axis=1, keepdims=True)

    scale = lax.rsqrt(lax.fori_loop(0, fold, squares, zero) * (1.0 / ff) + EPS)

    def middle(j, carry):
        total, up_sum, cross_sum = carry
        plain = (gelu[j] - center) * scale
        inner = (plain * broad[1, j] + broad[2, j]).astype(BF)
        total = total + mm(inner, down_w[j])
        grads = dot_cols(cot[...], down_w[j])
        put_down(j, dot_rows(inner, cot[...]))
        broad_g[1, j] = jnp.sum(grads * plain, axis=0, keepdims=True)
        broad_g[2, j] = jnp.sum(grads, axis=0, keepdims=True)
        up = grads * broad[1, j]
        inner_g[j] = up
        up_sum = up_sum + jnp.sum(up, axis=1, keepdims=True)
        cross_sum = cross_sum + jnp.sum(up * plain, axis=1, keepdims=True)
        return total, up_sum, cross_sum

    start = hidden + narrow[5:6]
    total, up_sum, cross_sum = lax.fori_loop(0, fold, middle, (start, zero, zero))
    output[...] = total.astype(BF)
    up_mean = up_sum * (1.0 / ff)
    cross_mean = cross_sum * (1.0 / ff)

    def back(j, total):
        plain = (gelu[j] - center) * scale
        grads = ((inner_g[j] - up_mean - plain * cross_mean) * scale * slope[j]).astype(BF)
        broad_g[0, j] = jnp.sum(grads.astype(F32), axis=0, keepdims=True)
        put_up(j, dot_rows(feed_in, grads))
        return total + dot_cols(grads, up_w[j])

    feed_grads = lax.fori_loop(0, fold, back, jnp.zeros((rows, width), F32))
    cot_wide = cot[...].astype(F32)
    got, feed_gain_g, feed_shift_g = norm_back(
        feed_grads, narrow[3:4], feed_plain, feed_scale, width
    )
    hidden_g = cot_wide + got
    hidden_grad[...] = hidden_g
    branch = hidden_g.astype(BF)
    put_out(dot_rows(branch, mixed))
    mixed_g, attn_gain_g, attn_shift_g = norm_back(
        dot_cols(branch, out_w[...]), narrow[0:1], attn_plain, attn_scale, width
    )
    turned = mixed_g.astype(BF).T
    mine, other = swap_if(core, turned[: 2 * cols], turned[2 * cols :])
    gone[...] = jnp.concatenate(swap_if(cross, other[:cols], other[cols:]), axis=0)
    kept[...], kept_away[...] = swap_if(cross, mine[:cols], mine[cols:])
    narrow_g[0:1] = jnp.sum(cot_wide, axis=0, keepdims=True)
    narrow_g[1:2] = feed_gain_g
    narrow_g[2:3] = feed_shift_g
    narrow_g[3:4] = jnp.sum(branch.astype(F32), axis=0, keepdims=True)
    narrow_g[4:5] = attn_gain_g
    narrow_g[5:6] = attn_shift_g
    narrow_g[6:8] = jnp.zeros((2, width), F32)


def prepare_kernel(plan, group, facts, q, kept, near, far, last, combined, lse, *refs):
    refs = list(refs)
    cross, core = sides(facts, group)
    mine = join_if(core, kept[0], near[0], 1)
    other = join_if(core, far[0], last[0], 1)
    g = join_if(cross, mine, other, 1)
    strides = [1] + [s.stride for s in plan.spaces]
    extras = {s: refs.pop(0) for s in strides}
    outs = {s: (refs.pop(0), refs.pop(0), refs.pop(0)) for s in strides}
    head = pl.program_id(0)
    total = -lse[0, 0:1]
    dots = -jnp.sum(g.astype(F32) * combined[0], axis=0, keepdims=True)
    stats = jnp.concatenate([stat_rows(total, 16), stat_rows(dots, 16)], axis=0)
    stack = jnp.concatenate([q[0], g, stats], axis=0)
    held = {1: stack}
    for stride in strides:
        if stride > 1:
            space = plan.space(stride)
            source = held[1] if stride == 2 else held[2]
            held[stride] = lanes_down(space, first_in(facts, head, stride), source).astype(BF)
        mine = held[stride]
        queries, grads, rows = outs[stride]
        stat = mine[2 * HALF :].astype(F32)
        extra = extras[stride][0].astype(F32)
        row = lax.broadcasted_iota(jnp.int32, extra.shape, 0)
        low = jnp.zeros_like(extra)
        for j in range(3):
            extra = jnp.where(row == LSE_ROW + j, stat[j : j + 1], extra)
            low = jnp.where(row == j, stat[16 + j : 17 + j], low)
        queries[0] = jnp.concatenate([mine[:HALF], extra.astype(BF)], axis=0)
        grads[0] = jnp.concatenate([low.astype(BF), mine[HALF : 2 * HALF]], axis=0)
        rows[0] = mine[: 2 * HALF].T


def space_back(plan, space, refs, extra_k, queries, grads, rows, out_q, out_refs):
    sources = space_sources(plan, space, refs)
    targets = space_sources(plan, space, out_refs)
    packet = jnp.concatenate([ref[0, at : at + space.keys] for level, ref, at in sources], axis=0)
    keys_extra = with_extra(packet, extra_k)
    values_ones = with_ones(packet)
    keys_turned = packet.T[:HALF]
    block = min(512, space.queries)
    pair = None
    for start in range(0, space.queries, block):
        stop = start + block
        got, turned = attend_back(
            keys_extra,
            values_ones,
            keys_turned,
            queries[:, start:stop],
            grads[:, start:stop],
            rows[start:stop],
        )
        pair = got if pair is None else pair + got
        out_q[:, start:stop] = turned
    for j, (level, ref, at) in enumerate(targets):
        ref[0, at : at + space.keys] = pair[j * space.keys : (j + 1) * space.keys].astype(BF)


def spaces_back_kernel(plan, group, spaces, levels, facts, *refs):
    refs = list(refs)
    packets = {lv: [refs.pop(0) for _ in plan.masks(lv)] for lv in levels}
    ins = {s.stride: [refs.pop(0) for _ in range(4)] for s in spaces}
    outs = {lv: [refs.pop(0) for _ in plan.masks(lv)] for lv in levels}
    out_q = {s.stride: refs.pop(0) for s in spaces}
    for space in spaces:
        flag = reach_flag(plan, facts, group, space)

        @pl.when(flag > 0)
        def _(space=space):
            extra_k, queries, grads, rows = [r[0] for r in ins[space.stride]]
            space_back(
                plan,
                space,
                packets,
                extra_k,
                queries,
                grads,
                rows,
                out_q[space.stride].at[0],
                outs,
            )

        @pl.when(flag == 0)
        def _(space=space):
            out_q[space.stride][...] = jnp.zeros_like(out_q[space.stride])
            for level, ref, at in space_sources(plan, space, outs):
                ref[0, at : at + space.keys] = jnp.zeros((space.keys, 128), BF)


def own_back_kernel(plan, block, kv, extra_k, queries, grads, rows, pair, out_q):
    keys_extra = with_extra(kv[0], extra_k[0])
    values_ones = with_ones(kv[0])
    keys_turned = kv[0].T[:HALF]
    for start in reversed(range(0, plan.window, block)):
        stop = start + block
        got, turned = attend_back(
            keys_extra[:stop],
            values_ones[:stop],
            keys_turned[:, :stop],
            queries[0, :, start:stop],
            grads[0, :, start:stop],
            rows[0, start:stop],
            block,
        )
        if stop == plan.window:
            pair[0] = got
        else:
            pair[0, :stop] += got
        out_q[0, :, start:stop] = turned


def gather_kernel(plan, group, facts, pair, own_q, *refs):
    refs = list(refs)
    queries = {s.stride: refs.pop(0) for s in plan.spaces}
    returns = {lv: refs.pop(0) for lv in plan.levels}
    out_pair, out_q = refs
    head = pl.program_id(0)
    near = plan.spaces[0]
    rows_two = jnp.zeros((near.keys, 128), F32)
    lanes_two = queries[2][0]
    for space in plan.spaces:
        first = first_in(facts, head, space.stride)
        total = None
        for level in space.levels:
            at = plan.packet[level][0][space.stride]
            got = returns[level][0, at : at + space.keys]
            if space.stride == 2:
                rows_two = rows_two + got.astype(F32)
            else:
                rows_two = rows_two + rows_up(space, first, got)
        if space.stride != 2:
            lanes_two = lanes_two + wide_up(space, first, queries[space.stride][0])
    first = first_in(facts, head, 2)
    high, low = split_two(rows_two)
    got = rows_up(near, first, jnp.concatenate([high, low], axis=1))
    out_pair[...] = (pair[0] + got[:, :128] + got[:, 128:]).astype(BF)
    out_q[0] = (own_q[0] + wide_up(near, first, lanes_two)).astype(BF)


def per_head(rows, cols):
    return pl.BlockSpec((1, rows, cols), lambda h: (h, 0, 0))


def head_call(kernel, group, facts, ins, outs, scratch=(), cost=0, specs=None):
    in_specs = [per_head(*a.shape[1:]) for a in ins]
    out_specs = [per_head(r, c) for r, c, d in outs]
    shapes = [jax.ShapeDtypeStruct((group, r, c), d) for r, c, d in outs]
    for j, (spec, shape) in (specs or {}).items():
        out_specs[j], shapes[j] = spec, shape
    moved = sum(a.size * a.dtype.itemsize for a in ins)
    front = [] if facts is None else [facts]
    return pl.pallas_call(
        kernel,
        grid=(group,),
        in_specs=[pl.BlockSpec(memory_space=pltpu.SMEM)] * len(front) + in_specs,
        out_specs=out_specs,
        out_shape=shapes,
        scratch_shapes=list(scratch),
        compiler_params=pltpu.CompilerParams(vmem_limit_bytes=VMEM_LIMIT),
        cost_estimate=pl.CostEstimate(flops=cost, bytes_accessed=moved, transcendentals=0),
    )(*front, *ins)


def swap(array, axis, bit, only=lambda i: True):
    count = lax.axis_size(axis)
    return lax.ppermute(array, axis, [(i, i ^ bit) for i in range(count) if only(i)])


def level_jump(plan, level, packet):
    step = 1 << level
    pairs = [(i, i + step) for i in range(plan.seq_count) if not i & step]
    return lax.ppermute(packet, "seq", pairs)


def level_hop(plan, level, found, hop):
    bit = level - 2 - hop
    if bit >= 0:
        found += [swap(f, "seq", 2 << bit, lambda i: i & (1 << level)) for f in found]


def level_return(plan, level, grads):
    step = 1 << level
    for bit in range(level - 1):
        half = len(grads) // 2
        got = [swap(g, "seq", 2 << bit, lambda i: i & step) for g in grads[half:]]
        grads = [(a.astype(F32) + b.astype(F32)).astype(BF) for a, b in zip(grads[:half], got)]
    pairs = [(i + step, i) for i in range(plan.seq_count) if not i & step]
    return lax.ppermute(grads[0], "seq", pairs)


def in_order(bit, mine, other, axis):
    zero = bit == 0
    first = jnp.where(zero, mine, other)
    second = jnp.where(zero, other, mine)
    return jnp.concatenate([first, second], axis=axis)


def pick_half(array, index, axis):
    half = array.shape[axis] // 2
    return lax.dynamic_slice_in_dim(array, index * half, half, axis)


def per_device(
    tokens,
    mix_gain,
    mix_shift,
    query_weight,
    query_bias,
    key_weight,
    value_weight,
    value_bias,
    attn_gain,
    attn_shift,
    out_weight,
    out_bias,
    feed_gain,
    feed_shift,
    up_weight,
    up_bias,
    inner_gain,
    inner_shift,
    down_weight,
    down_bias,
    cotangent,
):
    tok_rows, width = tokens.shape
    seq_count = lax.axis_size("seq")
    devices = seq_count * lax.axis_size("head")
    plan = Plan(tok_rows, seq_count)
    seq_index = lax.axis_index("seq")
    core = lax.axis_index("head")
    cross = seq_index % 2
    window_index = seq_index // 2
    heads_here = query_weight.shape[1] // HEAD_DIM
    group = heads_here // 2
    cols = group * HEAD_DIM
    half_rows = tok_rows // 2
    heads = core * heads_here + cross * group + jnp.arange(group, dtype=jnp.int32)
    ff = up_weight.shape[1]

    tokens_half = pick_half(tokens, core, 0)
    tokens_half, up_weight, down_weight, out_weight, small = lax.optimization_barrier(
        (
            tokens_half,
            up_weight,
            down_weight,
            out_weight,
            [up_bias, inner_gain, inner_shift, feed_gain, feed_shift, down_bias],
        )
    )

    up_rows = up_weight.shape[0]
    fold = ff // width
    down_rows = down_weight.shape[0]
    small = jnp.concatenate(small)
    small_at = [down_rows, down_rows, down_rows, up_rows, up_rows, up_rows]
    pad = -small.shape[0] % width
    small_rows = jnp.pad(small, (0, pad)).reshape(-1, width)
    up_packed = jnp.concatenate(
        [up_weight[:, j * width : (j + 1) * width] for j in range(fold)], axis=0
    )
    packed = jnp.concatenate([up_packed, down_weight, small_rows], axis=0)
    packed = jnp.pad(packed, ((0, -packed.shape[0] % 16), (0, 0)))
    gathered = lax.all_gather(packed, BOTH, axis=0, tiled=False)

    got = swap(tokens_half, "seq", 1)
    other = swap(got, "head", 1)
    partner = in_order(core, got, other, 0)
    window_tokens = in_order(cross, tokens, partner, 0)
    out_extra = jnp.concatenate([attn_gain, attn_shift]).reshape(1, width)
    out_packed = jnp.concatenate([out_weight, jnp.pad(out_extra, ((0, 15), (0, 0)))], axis=0)
    out_other = swap(out_packed, "head", 1)
    out_full = in_order(core, out_packed[: width // 2], out_other[: width // 2], 0)
    gain_mine, gain_other = out_packed[width // 2], out_other[width // 2]
    attn_gain_full = in_order(core, gain_mine[: width // 2], gain_other[: width // 2], 0)
    attn_shift_full = in_order(core, gain_mine[width // 2 :], gain_other[width // 2 :], 0)

    firsts = [first_of(plan, s, window_index, heads) for s in (2, 4, 6, 12)]
    firsts = [firsts[0]] + [jnp.mod(f - firsts[0], s) // 2 for f, s in zip(firsts[1:], (4, 6, 12))]
    flags = jnp.stack([(window_index >> b) & 1 for b in range(4)])
    side = jnp.stack([cross, core])
    facts = jnp.concatenate([jnp.stack(firsts, axis=1).reshape(-1), flags, side])
    facts = facts.astype(jnp.int32)

    wq = pick_half(query_weight, cross, 1).T
    wk = pick_half(key_weight, cross, 1).reshape(width, group, HEAD_DIM)
    wv = pick_half(value_weight, cross, 1).reshape(width, group, HEAD_DIM)
    wkv = jnp.concatenate([wk, wv], axis=2).reshape(width, 2 * cols)
    bq = pick_half(query_bias, cross, 0).astype(F32).reshape(cols, 1)
    bv = pick_half(value_bias, cross, 0).astype(F32).reshape(group, HEAD_DIM)
    bkv = jnp.concatenate([jnp.zeros_like(bv), bv], axis=1).reshape(1, 2 * cols)
    mix_gain_wide = mix_gain.astype(F32).reshape(1, width)
    mix_shift_wide = mix_shift.astype(F32).reshape(1, width)

    whole = pl.BlockSpec(memory_space=pltpu.VMEM)
    packet_shapes = [
        jax.ShapeDtypeStruct((group, plan.packet[level][1], 128), BF) for level in plan.levels
    ]
    normed, queries_turned, pair_rows, *packets = pl.pallas_call(
        functools.partial(project_kernel, plan, group),
        in_specs=[pl.BlockSpec(memory_space=pltpu.SMEM)] + [whole] * 7,
        out_specs=[whole] * (3 + len(packet_shapes)),
        out_shape=[
            jax.ShapeDtypeStruct((plan.window, width), BF),
            jax.ShapeDtypeStruct((group, HEAD_DIM, plan.window), BF),
            jax.ShapeDtypeStruct((group, plan.window, 128), BF),
        ]
        + packet_shapes,
        compiler_params=pltpu.CompilerParams(vmem_limit_bytes=VMEM_LIMIT),
    )(facts, window_tokens, mix_gain_wide, mix_shift_wide, wq, bq, wkv, bkv)

    received = {lv: [level_jump(plan, lv, pk)] for lv, pk in zip(plan.levels, packets)}

    on = jnp.asarray(True)
    extra_k = {1: extra_keys(plan, 1, plan.window, window_index, heads, on)}
    extra_q = {1: extra_queries(plan, 1, plan.window, window_index, heads)}
    for space in plan.spaces:
        parts = []
        for level in space.levels:
            for mask in plan.masks(level):
                source = (window_index ^ mask) ^ (1 << (level - 1))
                on = flags[level - 1] == 1
                parts.append(extra_keys(plan, space.stride, space.keys, source, heads, on))
        extra_k[space.stride] = jnp.concatenate(parts, axis=1)
        extra_q[space.stride] = extra_queries(
            plan, space.stride, space.queries, window_index, heads
        )

    window = plan.window
    near, far = plan.spaces[0], plan.spaces[1:]
    block = 512
    out_own, lse_own = head_call(
        functools.partial(own_kernel, plan, block),
        group,
        None,
        [pair_rows, extra_k[1], queries_turned, extra_q[1]],
        [(HEAD_DIM, window, F32), (8, window, F32)],
        cost=4 * group * window * window * 128,
    )
    received, out_own, lse_own = lax.optimization_barrier((received, out_own, lse_own))
    for lv in plan.levels:
        level_hop(plan, lv, received[lv], 0)
    out_near, lse_near = head_call(
        functools.partial(near_kernel, plan, group),
        group,
        facts,
        [queries_turned, *received[1], extra_k[2], extra_q[2]],
        [(HEAD_DIM, near.queries, F32), (8, near.queries, F32)],
        cost=2 * group * window * window * 128,
    )
    up_full = jnp.stack(
        [
            gathered[:, j * up_rows : (j + 1) * up_rows].reshape(width, width)
            for j in range(fold)
        ]
    )
    down_at = fold * up_rows
    down_full = gathered[:, down_at : down_at + down_rows].reshape(fold, width, width)
    received, out_near, lse_near, up_full, down_full = lax.optimization_barrier(
        (received, out_near, lse_near, up_full, down_full)
    )
    for lv in plan.levels:
        for hop in range(1, lv - 1):
            level_hop(plan, lv, received[lv], hop)
    far_packets = [r for lv in plan.levels[1:] for r in received[lv]]
    far_extras = [e for s in far for e in (extra_k[s.stride], extra_q[s.stride])]
    scratch = []
    for s in far:
        scratch += [pltpu.VMEM((HEAD_DIM, s.queries), F32), pltpu.VMEM((8, s.queries), F32)]
    combined, lse_all, same, other, away = head_call(
        functools.partial(far_kernel, plan, group),
        group,
        facts,
        [queries_turned, out_own, lse_own, out_near, lse_near, *far_packets, *far_extras],
        [
            (HEAD_DIM, window, F32),
            (8, window, F32),
            (HEAD_DIM, half_rows, BF),
            (HEAD_DIM, half_rows, BF),
            (HEAD_DIM, tok_rows, BF),
        ],
        scratch,
        cost=2 * group * window * window * 128,
    )

    across = swap(away, "seq", 1)
    beside = swap(other, "head", 1)
    beyond = swap(across[:, :, half_rows:], "head", 1)

    small_full = gathered[:, down_at + down_rows : down_at + down_rows + small_rows.shape[0]]
    small_full = small_full.reshape(devices, -1).astype(F32)
    pieces, at = [], 0
    for size in small_at:
        pieces.append(small_full[:, at : at + size].reshape(-1))
        at += size
    up_bias_w, inner_gain_w, inner_shift_w, feed_gain_w, feed_shift_w, down_bias_w = pieces

    narrow = [attn_gain_full, attn_shift_full, out_bias, feed_gain_w, feed_shift_w, down_bias_w]
    narrow = jnp.stack([v.astype(F32) for v in narrow])
    broad = jnp.stack([up_bias_w, inner_gain_w, inner_shift_w]).reshape(3, fold, 1, width)
    feed_ins = [
        same.reshape(cols, half_rows),
        across.reshape(cols, tok_rows),
        beside.reshape(cols, half_rows),
        beyond.reshape(cols, half_rows),
        tokens_half,
        cotangent,
        out_full,
        up_full,
        down_full,
        narrow,
        broad,
    ]
    rows_wide = (half_rows, width)
    shapes = [
        (rows_wide, BF),
        (rows_wide, F32),
        ((2 * cols, half_rows), BF),
        ((cols, half_rows), BF),
        ((cols, half_rows), BF),
        ((3, fold, 1, width), F32),
        ((8, width), F32),
    ]
    shares = Shares(devices, width, ff)
    if shares.direct:
        shapes += [((devices, shares.rows, width // 2), BF)]
    else:
        shapes += [((fold, width, width), BF), ((fold, width, width), BF), ((width, width), BF)]
    (
        output,
        hidden_grad,
        gone,
        kept_away,
        kept,
        broad_grads,
        narrow_grads,
        *stack,
    ) = pl.pallas_call(
        functools.partial(feed_kernel, group, fold, shares, shares.direct),
        in_specs=[pl.BlockSpec(memory_space=pltpu.SMEM)] + [whole] * len(feed_ins),
        out_specs=[whole] * len(shapes),
        out_shape=[jax.ShapeDtypeStruct(shape, dtype) for shape, dtype in shapes],
        scratch_shapes=[pltpu.VMEM((fold, half_rows, width), F32)] * 3,
        compiler_params=pltpu.CompilerParams(vmem_limit_bytes=62 * 2**20),
        cost_estimate=pl.CostEstimate(
            flops=12 * half_rows * width * ff, bytes_accessed=2**25, transcendentals=0
        ),
    )(facts, *feed_ins)
    up_bias_grad, inner_gain_grad, inner_shift_grad = broad_grads.reshape(3, ff)
    down_bias_grad, feed_gain_grad, feed_shift_grad = narrow_grads[0:3]
    out_bias_grad, attn_gain_grad, attn_shift_grad = narrow_grads[3:6]

    by_device = [up_bias_grad, inner_gain_grad, inner_shift_grad, down_bias_grad]
    by_device += [feed_gain_grad, feed_shift_grad, out_bias_grad]
    by_core = [attn_gain_grad, attn_shift_grad]
    small_grads = [g.reshape(devices, -1) for g in by_device]
    small_grads += [
        g.reshape(2, seq_count, -1).transpose(1, 0, 2).reshape(devices, -1) for g in by_core
    ]
    small_sizes = [g.shape[1] for g in small_grads]
    small_grads = shares.small(small_grads)
    stack = stack[0] if shares.direct else shares.stack(*stack)
    stack = lax.dynamic_update_slice(stack, small_grads.astype(BF), (0, shares.small_at, 0))
    summed = lax.psum_scatter(
        stack.reshape(-1, width // 2), BOTH, scatter_dimension=0, tiled=True
    )

    near_grads = swap(gone, "head", 1)
    far_grads = swap(kept_away, "seq", 1)
    last_grads = swap(near_grads[cols:], "seq", 1)
    grad_pieces = [kept, near_grads[:cols], far_grads, last_grads]
    grad_pieces = [g.reshape(group, HEAD_DIM, half_rows) for g in grad_pieces]

    strides = [1] + [s.stride for s in plan.spaces]
    counts = [window] + [s.queries for s in plan.spaces]
    prepared = head_call(
        functools.partial(prepare_kernel, plan, group),
        group,
        facts,
        [queries_turned, *grad_pieces, combined, lse_all, *[extra_q[s] for s in strides]],
        [o for n in counts for o in ((128, n, BF), (128, n, BF), (n, 128, BF))],
    )
    prepared = {s: prepared[3 * j : 3 * j + 3] for j, s in enumerate(strides)}

    def back(spaces, levels, cost):
        ins = [r for lv in levels for r in received[lv]]
        shapes = [(r.shape[1], 128, BF) for r in ins]
        for s in spaces:
            ins += [extra_k[s.stride], *prepared[s.stride]]
        shapes += [(HEAD_DIM, s.queries, F32) for s in spaces]
        outs = head_call(
            functools.partial(spaces_back_kernel, plan, group, spaces, levels),
            group,
            facts,
            ins,
            shapes,
            cost=cost,
        )
        pairs, at = {}, 0
        for lv in levels:
            pairs[lv] = list(outs[at : at + len(received[lv])])
            at += len(received[lv])
        return pairs, list(outs[at:])

    far_pairs, far_queries = back(far, plan.levels[1:], 5 * group * window * window * 128)
    returned = {lv: level_return(plan, lv, far_pairs[lv]) for lv in plan.levels[1:]}
    near_pairs, near_queries = back([near], [1], 5 * group * window * window * 128)
    returned[1] = level_return(plan, 1, near_pairs[1])
    own_pair, own_q = head_call(
        functools.partial(own_back_kernel, plan, 256),
        group,
        None,
        [pair_rows, extra_k[1], *prepared[1]],
        [(window, 128, F32), (HEAD_DIM, window, F32)],
        cost=10 * group * window * window * 128,
    )
    pair_spec = pl.BlockSpec((window, 128), lambda h: (0, h))
    pair_shape = jax.ShapeDtypeStruct((window, group * 128), BF)
    pair_low, query_low = head_call(
        functools.partial(gather_kernel, plan, group),
        group,
        facts,
        [own_pair, own_q, *near_queries, *far_queries, *[returned[lv] for lv in plan.levels]],
        [(window, 128, BF), (HEAD_DIM, window, BF)],
        specs={0: (pair_spec, pair_shape)},
    )
    query_low = query_low.reshape(cols, window)

    part = dot_rows(query_low, wq) + dot_cols(pair_low, wkv)
    tokens_wide = window_tokens.astype(F32)
    center = jnp.mean(tokens_wide, axis=1, keepdims=True)
    centered = tokens_wide - center
    spread = jnp.mean(centered * centered, axis=1, keepdims=True)
    plain = centered * lax.rsqrt(spread + EPS)
    mix_part = jnp.concatenate([jnp.sum(part * plain, axis=0), jnp.sum(part, axis=0)])
    part_low = part.astype(BF).reshape(2, 2, half_rows, width)
    mine = lax.dynamic_index_in_dim(part_low, core, 1, keepdims=False)
    away = lax.dynamic_index_in_dim(part_low, 1 - core, 1, keepdims=False)
    got = swap(away, "head", 1)
    both = (mine.astype(F32) + got.astype(F32)).astype(BF)
    near_part = lax.dynamic_index_in_dim(both, cross, 0, keepdims=False)
    away = lax.dynamic_index_in_dim(both, 1 - cross, 0, keepdims=False)
    away_got = swap(away, "seq", 1)
    weight_part = jnp.concatenate(
        [dot_rows(normed, pair_low), dot_cols(normed.T, query_low)], axis=1
    ).astype(BF)
    pair_sums = jnp.sum(pair_low.astype(F32), axis=0)
    query_sums = jnp.sum(query_low.astype(F32), axis=1)
    sums = jnp.concatenate([pair_sums, query_sums, mix_part])
    sums_pad = -sums.shape[0] % 1024
    sums = jnp.pad(sums, (0, sums_pad)).reshape(-1, 128)
    block_rows = width // seq_count
    weight_part = weight_part.reshape(seq_count // 2, 2 * block_rows, 3 * cols)
    bits = (seq_count // 2).bit_length() - 1
    for bit in range(bits):
        here = (window_index >> bit) & 1
        pairs = weight_part.reshape(-1, 2, 2 * block_rows, 3 * cols)
        mine = lax.dynamic_index_in_dim(pairs, here, 1, keepdims=False)
        got = lax.dynamic_index_in_dim(pairs, 1 - here, 1, keepdims=False)
        got = swap(got, "seq", 2 << bit)
        weight_part = (mine.astype(F32) + got.astype(F32)).astype(BF)
        sums = sums + swap(sums, "seq", 2 << bit)
    weight_part, sums, away_got = lax.optimization_barrier((weight_part, sums, away_got))
    normed_grad = near_part.astype(F32) + away_got.astype(F32)
    tokens_norm_grad = jax.vjp(
        layer_norm, tokens_half.astype(F32), mix_gain.astype(F32), mix_shift.astype(F32)
    )[1](normed_grad)[0]
    tokens_grad = hidden_grad + tokens_norm_grad
    weight_part = weight_part[0]
    got = swap(pick_half(weight_part, 1 - cross, 0), "seq", 1)
    mine = pick_half(weight_part, cross, 0)
    sums_other = swap(sums, "seq", 1)
    flat, flat_other = sums.reshape(-1), sums_other.reshape(-1)
    mix_sum = flat[3 * cols : 3 * cols + 2 * width] + flat_other[3 * cols : 3 * cols + 2 * width]
    mix_sum = mix_sum.reshape(-1, 128)
    mix_sum = (mix_sum + swap(mix_sum, "head", 1)).reshape(2, devices, -1)
    mix_sum = lax.dynamic_index_in_dim(mix_sum, seq_index * 2 + core, 1, keepdims=False)

    def parts_of(array):
        pair = array[..., : 2 * cols].reshape(array.shape[:-1] + (group, 2, HEAD_DIM))
        key, value = pair[..., 0, :], pair[..., 1, :]
        lead = array.shape[:-1] + (cols,)
        return array[..., 2 * cols : 3 * cols], key.reshape(lead), value.reshape(lead)

    weight_grads = [
        in_order(cross, a, b, 1).astype(F32) for a, b in zip(parts_of(mine), parts_of(got))
    ]
    bias_grads = [
        lax.dynamic_index_in_dim(
            in_order(cross, a, b, 0).reshape(seq_count, -1), seq_index, 0, keepdims=False
        )
        for a, b in zip(parts_of(flat[: 3 * cols]), parts_of(flat_other[: 3 * cols]))
    ]

    span, step = shares.up_span, down_rows
    up_sum = [summed[p * span : p * span + up_rows] for p in range(2 * fold)]
    up_sum = jnp.concatenate(up_sum, axis=1).astype(F32)
    down_sum = summed[shares.down_at : shares.out_at].reshape(2, step, width // 2)
    down_sum = jnp.concatenate([down_sum[0], down_sum[1]], axis=1).astype(F32)
    out_sum = summed[shares.out_at : shares.small_at].T.astype(F32)
    flat_small = summed[shares.small_at : shares.small_at + small_grads.shape[1]]
    flat_small = flat_small.reshape(-1).astype(F32)
    smalls, place = [], 0
    for size in small_sizes:
        smalls.append(flat_small[place : place + size])
        place += size
    (
        up_bias_sum,
        inner_gain_sum,
        inner_shift_sum,
        down_bias_sum,
        feed_gain_sum,
        feed_shift_sum,
        out_bias_sum,
        attn_gain_sum,
        attn_shift_sum,
    ) = smalls
    return (
        output,
        tokens_grad,
        mix_sum[0],
        mix_sum[1],
        weight_grads[0],
        bias_grads[0],
        weight_grads[1],
        weight_grads[2],
        bias_grads[2],
        attn_gain_sum,
        attn_shift_sum,
        out_sum,
        out_bias_sum,
        feed_gain_sum,
        feed_shift_sum,
        up_sum,
        up_bias_sum,
        inner_gain_sum,
        inner_shift_sum,
        down_sum,
        down_bias_sum,
    )


def solution(mesh):
    return jax.shard_map(
        per_device,
        mesh=mesh,
        in_specs=(
            P("seq", None),
            P(),
            P(),
            P(None, "head"),
            P("head"),
            P(None, "head"),
            P(None, "head"),
            P("head"),
            P("head"),
            P("head"),
            P("head", None),
            P(),
            P(("seq", "head")),
            P(("seq", "head")),
            P(("seq", "head"), None),
            P(("seq", "head")),
            P(("seq", "head")),
            P(("seq", "head")),
            P(("seq", "head"), None),
            P(("seq", "head")),
            P(("seq", "head"), None),
        ),
        out_specs=(
            P(("seq", "head"), None),
            P(("seq", "head"), None),
            P(("seq", "head")),
            P(("seq", "head")),
            P("seq", "head"),
            P(("head", "seq")),
            P("seq", "head"),
            P("seq", "head"),
            P(("head", "seq")),
            P(("head", "seq")),
            P(("head", "seq")),
            P("head", "seq"),
            P(("seq", "head")),
            P(("seq", "head")),
            P(("seq", "head")),
            P(("seq", "head"), None),
            P(("seq", "head")),
            P(("seq", "head")),
            P(("seq", "head")),
            P(("seq", "head"), None),
            P(("seq", "head")),
        ),
        check_vma=False,
    )
```
